256 devices in a mesh: occ: 8 (over y, x_lo), vir: 32 (over z, x_hi, core).
Axes of the slice: x: 4 (x_hi: 2, x_lo: 2; x = x_hi * 2 + x_lo), y: 4, z: 8, core: 2. Of those that a mesh axis runs over, the one named last changes fastest.
Arguments:
- b_factors: float32 [64, 1024, 4096], P('occ', 'vir'), may hold values from -0.6 to 0.6
- occ_energy: float32 [64], replicated, may hold values from -2 to -0.3
- vir_energy: float32 [1024], replicated, may hold values from 0.2 to 3
Outputs:
- gamma: float32 [64, 1024, 4096], P('occ', 'vir')
The draws below stay inside these ranges and needn't reach their ends.
All inputs are finite; a program needn't handle non-finite values.
Results may differ from the reference program's by a relative error of at most 0.0003.
Values sent between devices are 32-bit elements; how exact they have to be, the bound alone decides.
No kernel may reach another device: no remote copies, remote signals or barrier semaphores. Data moves between devices by JAX's collectives and lax.ppermute only.
A program may use at most 128 MiB of HBM per device.

```python
import jax
import jax.numpy as jnp
from jax import lax

P_SIZE = 4096
OCC_DEV = 8
VIR_DEV = 32
O = 64
V = 1024
N_OCC = 8
N_VIR = 32


def steps_of(own_key, extent, pieces, smallest, top_value):
    loudness, own = 1.0, jax.random.fold_in(own_key, 6)
    for axis_at, blocks in pieces:
        steps = jnp.exp(jax.random.uniform(jax.random.fold_in(own, axis_at), (blocks,), jnp.float32, smallest / len(pieces), top_value / len(pieces)))
        loudness = loudness * jnp.repeat(steps, extent[axis_at] // blocks).reshape([-1 if axis == axis_at else 1 for axis in range(len(extent))])
    return loudness


def bell_draw(stream_key, dims, spread, bound, pieces=(), kind=jnp.bfloat16):
    values = spread * jax.random.normal(stream_key, dims, jnp.float32)
    if pieces:
        values = values * steps_of(stream_key, dims, pieces, -0.22, 0.18)
    return jnp.clip(values, -bound, bound).astype(kind)


def setup_inputs(seed: int = 0) -> dict:
    key_list = jax.random.split(jax.random.key(seed), 4)
    b_factors = bell_draw(key_list[0], (O, V, P_SIZE), 0.1, 0.6, ((0, 8), (1, 32)), jnp.float32)
    occ_energy = jnp.clip(jax.random.uniform(key_list[1], (O,), jnp.float32, -2.0, -0.3), -2.0, -0.3)
    vir_energy = jnp.clip(jax.random.uniform(key_list[2], (V,), jnp.float32, 0.2, 3.0), 0.2, 3.0)
    return {"b_factors": b_factors, "occ_energy": occ_energy, "vir_energy": vir_energy}


def reference(b_factors, occ_energy, vir_energy):
    rows = OCC_DEV * VIR_DEV
    width = b_factors.shape[2]
    blocks = b_factors.reshape(N_OCC, OCC_DEV, N_VIR, VIR_DEV, width).transpose(0, 2, 1, 3, 4).reshape(N_OCC, N_VIR, rows, width)
    gaps = (occ_energy[:, None] - vir_energy[None, :]).reshape(N_OCC, OCC_DEV, N_VIR, VIR_DEV).transpose(0, 2, 1, 3).reshape(N_OCC, N_VIR, rows)
    offsets = [(0, 0), (1, 0), (-1, 0), (0, 1), (0, -1)]
    high = lax.Precision.HIGHEST

    def one_block_row(index):
        mine = blocks[index]
        mine_gap = gaps[index]
        total = jnp.zeros_like(mine)
        for shift_occ, shift_vir in offsets:
            other_index = (index + shift_occ) % N_OCC
            other = jnp.roll(blocks[other_index], -shift_vir, axis=0)
            other_gap = jnp.roll(gaps[other_index], -shift_vir, axis=0)
            integral = jnp.einsum("vrp,vsp->vrs", mine, other, precision=high)
            amplitude = integral / (mine_gap[:, :, None] + other_gap[:, None, :])
            total = total + jnp.einsum("vrs,vsp->vrp", amplitude, other, precision=high)
        return total

    result = lax.map(one_block_row, jnp.arange(N_OCC, dtype=jnp.int32))
    return result.reshape(N_OCC, N_VIR, OCC_DEV, VIR_DEV, width).transpose(0, 2, 1, 3, 4).reshape(N_OCC * OCC_DEV, N_VIR * VIR_DEV, width)
```

```python
import functools
import jax
import jax.numpy as jnp
from jax import lax
from jax.experimental import pallas as pl
from jax.experimental.pallas import tpu as pltpu
from jax.sharding import PartitionSpec as P

AXES = ("occ", "vir")
PANEL = 512
NT = (((1,), (1,)), ((), ()))
NN = (((1,), (0,)), ((), ()))


def mxu(left, right, dims=NN):
    return lax.dot_general(left, right, dims, preferred_element_type=jnp.float32)


def halves(value):
    high = value.astype(jnp.bfloat16)
    low = (value - high.astype(jnp.float32)).astype(jnp.bfloat16)
    return high, low


def panels(width):
    return [slice(at, at + PANEL) for at in range(0, width, PANEL)]


def own_kernel(mine_ref, gap_row_ref, gap_col_ref, high_ref, low_ref, gamma_ref):
    rows, width = mine_ref.shape
    integral = jnp.zeros((rows, rows), jnp.float32)
    cross = jnp.zeros((rows, rows), jnp.float32)
    for cols in panels(width):
        high, low = halves(mine_ref[:, cols])
        high_ref[:, cols] = high
        low_ref[:, cols] = low
        integral += mxu(high, high, NT)
        cross += mxu(high, low, NT)
    integral = integral + (cross + cross.T)
    a_high, a_low = halves(integral / (gap_row_ref[...] + gap_col_ref[...]))
    for cols in panels(width):
        high, low = high_ref[:, cols], low_ref[:, cols]
        gamma_ref[:, cols] = mxu(a_high, high) + mxu(a_high, low) + mxu(a_low, high)


def visit_kernel(count, *refs):
    others = refs[:count]
    high_ref, low_ref, gap_row_ref, gap_col_ref, start_ref, gamma_ref, both_ref = refs[count:]
    rows, width = high_ref.shape
    extent = sum(ref.shape[0] for ref in others)
    main = jnp.zeros((rows, 2 * extent), jnp.float32)
    rest = jnp.zeros((rows, extent), jnp.float32)
    for cols in panels(width):
        high, low = halves(jnp.concatenate([ref[:, cols] for ref in others], axis=0))
        both = jnp.concatenate([high, low], axis=0)
        both_ref[:, cols] = both
        main += mxu(high_ref[:, cols], both, NT)
        rest += mxu(low_ref[:, cols], high, NT)
    integral = main[:, :extent] + (main[:, extent:] + rest)
    a_high, a_low = halves(integral / (gap_row_ref[...] + gap_col_ref[...]))
    a_twice = jnp.concatenate([a_high, a_high], axis=1)
    for cols in panels(width):
        both = both_ref[:, cols]
        gamma_ref[:, cols] = start_ref[:, cols] + (mxu(a_twice, both) + mxu(a_low, both[:extent]))


VMEM = pl.BlockSpec(memory_space=pltpu.VMEM)


def cost(rows, extent, width):
    return pl.CostEstimate(flops=12 * rows * extent * width, bytes_accessed=4 * extent * width, transcendentals=0)


def own_call(mine, gap_row, gap_col):
    rows, width = mine.shape
    return pl.pallas_call(
        own_kernel,
        out_shape=(
            jax.ShapeDtypeStruct((rows, width), jnp.bfloat16),
            jax.ShapeDtypeStruct((rows, width), jnp.bfloat16),
            jax.ShapeDtypeStruct((rows, width), jnp.float32),
        ),
        in_specs=[VMEM] * 3,
        out_specs=(VMEM,) * 3,
        compiler_params=pltpu.CompilerParams(vmem_limit_bytes=24 << 20),
        cost_estimate=cost(rows, rows, width),
        name="own_block",
    )(mine, gap_row, gap_col)


def visit_call(others, high, low, gap_row, gap_col, gamma, name):
    rows, width = gamma.shape
    extent = sum(other.shape[0] for other in others)
    return pl.pallas_call(
        functools.partial(visit_kernel, len(others)),
        out_shape=jax.ShapeDtypeStruct((rows, width), jnp.float32),
        in_specs=[VMEM] * (len(others) + 5),
        out_specs=VMEM,
        scratch_shapes=[pltpu.VMEM((2 * extent, width), jnp.bfloat16)],
        input_output_aliases={len(others) + 4: 0},
        compiler_params=pltpu.CompilerParams(vmem_limit_bytes=24 << 20),
        cost_estimate=cost(rows, extent, width),
        name=name,
    )(*others, high, low, gap_row, gap_col, gamma)


def local(b_factors, occ_energy, vir_energy):
    occ_block, vir_block, width = b_factors.shape
    occ_count = lax.axis_size("occ")
    vir_count = lax.axis_size("vir")
    occ_here = lax.axis_index("occ")
    vir_here = lax.axis_index("vir")

    def moved(block, target):
        route = []
        for occ in range(occ_count):
            for vir in range(vir_count):
                occ_to, vir_to = target(occ, vir)
                route.append(
                    (occ * vir_count + vir, occ_to % occ_count * vir_count + vir_to % vir_count)
                )
        return lax.ppermute(block, AXES, route)

    def across(occ, vir):
        return occ ^ 1, vir

    def along(occ, vir):
        return (occ - 2 if occ % 2 else occ + 2), vir

    def outward(occ, vir):
        return occ ^ 1, (vir + 1 if vir % 2 else vir - 1)

    def inward(occ, vir):
        return occ, vir ^ 1

    def gap_of(occ_place, vir_place):
        occ_part = lax.dynamic_slice_in_dim(
            occ_energy, occ_place % occ_count * occ_block, occ_block
        )
        vir_part = lax.dynamic_slice_in_dim(
            vir_energy, vir_place % vir_count * vir_block, vir_block
        )
        return occ_part[:, None] - vir_part[None, :]

    occ_side = 1 - 2 * (occ_here % 2)
    vir_side = 1 - 2 * (vir_here % 2)
    gap = gap_of(occ_here, vir_here)
    gap_inner = gap_of(occ_here, vir_here + vir_side)
    gap_near = gap_of(occ_here + occ_side, vir_here)
    gap_far = gap_of(occ_here + occ_count - occ_side, vir_here)
    gap_outer = gap_of(occ_here, vir_here + vir_count - vir_side)
    gap_row = gap.reshape(-1, 1)
    gap_step = jnp.concatenate([gap_near, gap_far, gap_outer], axis=1)

    def held(value, *earlier):
        return lax.optimization_barrier((value, earlier))[0]

    mine = b_factors.reshape(occ_block * vir_block, width)
    last = occ_block - 1
    near = [moved(b_factors[k], across) for k in range(2)]
    inner = moved(b_factors, inward)
    high, low, gamma = own_call(mine, gap_row, gap.reshape(1, -1))
    gamma_inner = visit_call(
        [inner.reshape(mine.shape)], high, low, gap_row, gap_inner.reshape(1, -1), gamma, "inner_block"
    )
    done = [gamma, gamma_inner]
    far, outer = [], []
    for k in range(occ_block):
        part = held(near[k], done[k])
        far.append(moved(part, along))
        outer.append(moved(part, outward))
        if k + 2 < occ_block:
            near.append(moved(held(b_factors[k + 2], part), across))
        if k > 0:
            others = [near[k - 1], far[k - 1], outer[k - 1]]
            others = [held(other, part) for other in others]
            done.append(
                visit_call(others, high, low, gap_row, gap_step[k - 1 : k], done[-1], "step_%d" % (k - 1))
            )
    gamma = visit_call(
        [near[last], far[last], outer[last]], high, low, gap_row, gap_step[last:], done[-1], "step_%d" % last
    )
    return gamma.reshape(occ_block, vir_block, width)


def solution(mesh):
    in_specs = (P("occ", "vir", None), P(), P())
    out_specs = P("occ", "vir", None)
    return jax.shard_map(local, mesh=mesh, in_specs=in_specs, out_specs=out_specs, check_vma=False)
```

```python
import functools
import jax
import jax.numpy as jnp
from jax import lax
from jax.experimental import pallas as pl
from jax.experimental.pallas import tpu as pltpu
from jax.sharding import PartitionSpec as P

AXES = ("occ", "vir")
PANEL = 512
NT = (((1,), (1,)), ((), ()))
NN = (((1,), (0,)), ((), ()))


def mxu(left, right, dims=NN):
    return lax.dot_general(left, right, dims, preferred_element_type=jnp.float32)


def halves(value):
    high = value.astype(jnp.bfloat16)
    low = (value - high.astype(jnp.float32)).astype(jnp.bfloat16)
    return high, low


def panels(width):
    return [slice(at, at + PANEL) for at in range(0, width, PANEL)]


def arriving(source_ref, stage_ref, sem):
    copies = []
    for at, cols in enumerate(panels(source_ref.shape[1])):
        copies.append(
            pltpu.make_async_copy(source_ref.at[:, cols], stage_ref.at[:, cols], sem.at[at])
        )
        copies[-1].start()
    return copies


def own_kernel(mine_ref, gap_row_ref, gap_col_ref, high_ref, low_ref, gamma_ref, stage_ref, sem):
    rows, width = mine_ref.shape
    copies = arriving(mine_ref, stage_ref, sem)
    integral = jnp.zeros((rows, rows), jnp.float32)
    cross = jnp.zeros((rows, rows), jnp.float32)
    for copy, cols in zip(copies, panels(width)):
        copy.wait()
        high, low = halves(stage_ref[:, cols])
        high_ref[:, cols] = high
        low_ref[:, cols] = low
        integral += mxu(high, high, NT)
        cross += mxu(high, low, NT)
    integral = integral + (cross + cross.T)
    a_high, a_low = halves(integral / (gap_row_ref[...] + gap_col_ref[...]))
    for cols in panels(width):
        high, low = high_ref[:, cols], low_ref[:, cols]
        gamma_ref[:, cols] = mxu(a_high, high) + mxu(a_high, low) + mxu(a_low, high)


def block_kernel(
    other_ref, high_ref, low_ref, gap_row_ref, gap_col_ref, start_ref, gamma_ref,
    other_high_ref, other_low_ref, stage_ref, sem,
):
    rows, width = high_ref.shape
    copies = arriving(other_ref, stage_ref, sem)
    integral = jnp.zeros((rows, rows), jnp.float32)
    for copy, cols in zip(copies, panels(width)):
        copy.wait()
        high, low = halves(stage_ref[:, cols])
        other_high_ref[:, cols] = high
        other_low_ref[:, cols] = low
        mine = high_ref[:, cols]
        integral += mxu(mine, high, NT) + (mxu(mine, low, NT) + mxu(low_ref[:, cols], high, NT))
    a_high, a_low = halves(integral / (gap_row_ref[...] + gap_col_ref[...]))
    for cols in panels(width):
        high, low = other_high_ref[:, cols], other_low_ref[:, cols]
        gamma_ref[:, cols] = start_ref[:, cols] + (
            mxu(a_high, high) + mxu(a_high, low) + mxu(a_low, high)
        )


def step_kernel(count, *refs):
    others = refs[:count]
    high_ref, low_ref, gap_row_ref, gap_col_ref, start_ref, gamma_ref, both_ref, *leaving = refs[count:]
    rows, width = high_ref.shape
    extent = sum(ref.shape[0] for ref in others)
    main = jnp.zeros((rows, 2 * extent), jnp.float32)
    rest = jnp.zeros((rows, extent), jnp.float32)
    for cols in panels(width):
        high, low = halves(jnp.concatenate([ref[:, cols] for ref in others], axis=0))
        both = jnp.concatenate([high, low], axis=0)
        both_ref[:, cols] = both
        main += mxu(high_ref[:, cols], both, NT)
        rest += mxu(low_ref[:, cols], high, NT)
    integral = main[:, :extent] + (main[:, extent:] + rest)
    a_high, a_low = halves(integral / (gap_row_ref[...] + gap_col_ref[...]))
    a_twice = jnp.concatenate([a_high, a_high], axis=1)
    copies = []
    for at, cols in enumerate(panels(width)):
        both = both_ref[:, cols]
        gamma = start_ref[:, cols] + (mxu(a_twice, both) + mxu(a_low, both[:extent]))
        if leaving:
            stage_ref, sem = leaving
            stage_ref[:, cols] = gamma
            copies.append(
                pltpu.make_async_copy(stage_ref.at[:, cols], gamma_ref.at[:, cols], sem.at[at])
            )
            copies[-1].start()
        else:
            gamma_ref[:, cols] = gamma
    for copy in copies:
        copy.wait()


VMEM = pl.BlockSpec(memory_space=pltpu.VMEM)
HBM = pl.BlockSpec(memory_space=pltpu.HBM)


def cost(rows, extent, width):
    return pl.CostEstimate(flops=12 * rows * extent * width, bytes_accessed=4 * extent * width, transcendentals=0)


def in_vmem(array):
    return pltpu.with_memory_space_constraint(array, pltpu.VMEM)


def in_hbm(array):
    return pltpu.with_memory_space_constraint(array, pltpu.HBM)


def stage(rows, width):
    return [pltpu.VMEM((rows, width), jnp.float32), pltpu.SemaphoreType.DMA((width // PANEL,))]


def own_call(mine, gap_row, gap_col):
    rows, width = mine.shape
    return pl.pallas_call(
        own_kernel,
        out_shape=(
            pltpu.VMEM((rows, width), jnp.bfloat16),
            pltpu.VMEM((rows, width), jnp.bfloat16),
            pltpu.VMEM((rows, width), jnp.float32),
        ),
        in_specs=[HBM, VMEM, VMEM],
        out_specs=(VMEM,) * 3,
        scratch_shapes=stage(rows, width),
        compiler_params=pltpu.CompilerParams(vmem_limit_bytes=12 << 20),
        cost_estimate=cost(rows, rows, width),
        name="own_block",
    )(in_hbm(mine), gap_row, gap_col)


def block_call(other, high, low, gap_row, gap_col, gamma):
    rows, width = gamma.shape
    half = pltpu.VMEM((rows, width), jnp.bfloat16)
    return pl.pallas_call(
        block_kernel,
        out_shape=pltpu.VMEM((rows, width), jnp.float32),
        in_specs=[HBM] + [VMEM] * 5,
        out_specs=VMEM,
        scratch_shapes=[half, half] + stage(rows, width),
        input_output_aliases={5: 0},
        compiler_params=pltpu.CompilerParams(vmem_limit_bytes=14 << 20),
        cost_estimate=cost(rows, rows, width),
        name="inner_block",
    )(in_hbm(other), in_vmem(high), in_vmem(low), gap_row, gap_col, in_vmem(gamma))


def step_call(others, high, low, gap_row, gap_col, gamma, name, final=False):
    rows, width = gamma.shape
    extent = sum(other.shape[0] for other in others)
    return pl.pallas_call(
        functools.partial(step_kernel, len(others)),
        out_shape=(pltpu.HBM if final else pltpu.VMEM)((rows, width), jnp.float32),
        in_specs=[VMEM] * (len(others) + 5),
        out_specs=HBM if final else VMEM,
        scratch_shapes=[pltpu.VMEM((2 * extent, width), jnp.bfloat16)]
        + (stage(rows, width) if final else []),
        input_output_aliases={} if final else {len(others) + 4: 0},
        compiler_params=pltpu.CompilerParams(vmem_limit_bytes=10 << 20),
        cost_estimate=cost(rows, extent, width),
        name=name,
    )(*map(in_vmem, others), in_vmem(high), in_vmem(low), gap_row, gap_col, in_vmem(gamma))


def local(b_factors, occ_energy, vir_energy):
    occ_block, vir_block, width = b_factors.shape
    occ_count = lax.axis_size("occ")
    vir_count = lax.axis_size("vir")
    occ_here = lax.axis_index("occ")
    vir_here = lax.axis_index("vir")

    def moved(block, target):
        route = []
        for occ in range(occ_count):
            for vir in range(vir_count):
                occ_to, vir_to = target(occ, vir)
                route.append(
                    (occ * vir_count + vir, occ_to % occ_count * vir_count + vir_to % vir_count)
                )
        return lax.ppermute(block, AXES, route)

    def across(occ, vir):
        return occ ^ 1, vir

    def along(occ, vir):
        return (occ - 2 if occ % 2 else occ + 2), vir

    def outward(occ, vir):
        return occ ^ 1, (vir + 1 if vir % 2 else vir - 1)

    def inward(occ, vir):
        return occ, vir ^ 1

    def gap_of(occ_place, vir_place):
        occ_part = lax.dynamic_slice_in_dim(
            occ_energy, occ_place % occ_count * occ_block, occ_block
        )
        vir_part = lax.dynamic_slice_in_dim(
            vir_energy, vir_place % vir_count * vir_block, vir_block
        )
        return occ_part[:, None] - vir_part[None, :]

    occ_side = 1 - 2 * (occ_here % 2)
    vir_side = 1 - 2 * (vir_here % 2)
    gap = gap_of(occ_here, vir_here)
    gap_inner = gap_of(occ_here, vir_here + vir_side)
    gap_near = gap_of(occ_here + occ_side, vir_here)
    gap_far = gap_of(occ_here + occ_count - occ_side, vir_here)
    gap_outer = gap_of(occ_here, vir_here + vir_count - vir_side)
    gap_row = gap.reshape(-1, 1)
    gap_step = jnp.concatenate([gap_near, gap_far, gap_outer], axis=1)

    def held(value, *earlier):
        return lax.optimization_barrier((value, earlier))[0]

    mine = b_factors.reshape(occ_block * vir_block, width)
    last = occ_block - 1
    parts = [b_factors[0]]
    for k in range(1, occ_block):
        parts.append(held(b_factors, parts[k - 1])[k])
    near = [moved(parts[k], across) for k in range(2)]
    inner = moved(held(b_factors, parts[1]), inward)
    high, low, gamma = own_call(held(mine, parts[1]), gap_row, gap.reshape(1, -1))
    gamma_inner = block_call(
        inner.reshape(mine.shape), high, low, gap_row, gap_inner.reshape(1, -1), gamma
    )
    done = [gamma, gamma_inner]
    far, outer = [], []
    for k in range(occ_block):
        part = held(near[k], done[k])
        far.append(moved(part, along))
        outer.append(moved(part, outward))
        if k + 2 < occ_block:
            near.append(moved(held(parts[k + 2], part), across))
        if k > 0:
            others = [near[k - 1], far[k - 1], outer[k - 1]]
            others = [held(other, part) for other in others]
            done.append(
                step_call(others, high, low, gap_row, gap_step[k - 1 : k], done[-1], "step_%d" % (k - 1))
            )
    gamma = step_call(
        [near[last], far[last], outer[last]], high, low, gap_row, gap_step[last:], done[-1], "step_%d" % last, True
    )
    return gamma.reshape(occ_block, vir_block, width)


def solution(mesh):
    in_specs = (P("occ", "vir", None), P(), P())
    out_specs = P("occ", "vir", None)
    return jax.shard_map(local, mesh=mesh, in_specs=in_specs, out_specs=out_specs, check_vma=False)
```

```python
import functools
import jax
import jax.numpy as jnp
from jax import lax
from jax.experimental import pallas as pl
from jax.experimental.pallas import tpu as pltpu
from jax.sharding import PartitionSpec as P

AXES = ("occ", "vir")
PANEL = 512
FIRST_INNER = 3
NT = (((1,), (1,)), ((), ()))
NN = (((1,), (0,)), ((), ()))


def mxu(left, right, dims=NN):
    return lax.dot_general(left, right, dims, preferred_element_type=jnp.float32)


def halves(value):
    high = value.astype(jnp.bfloat16)
    low = (value - high.astype(jnp.float32)).astype(jnp.bfloat16)
    return high, low


def panels(width):
    return [slice(at, at + PANEL) for at in range(0, width, PANEL)]


def fetch(source_ref, target_ref, sem):
    copy = pltpu.make_async_copy(source_ref, target_ref, sem)
    copy.start()
    return copy


def row_cuts(mine_ref, targets, first, sem):
    height = targets[0].shape[0]
    copies = []
    for at, target in enumerate(targets):
        rows = pl.ds((first + at) * height, height)
        copies.append(fetch(mine_ref.at[rows], target, sem.at[at]))
    return copies


def cut_kernel(count, mine_ref, *refs):
    for copy in row_cuts(mine_ref, refs[:count], 0, refs[count]):
        copy.wait()


def own_kernel(skip, mine_ref, gap_row_ref, gap_col_ref, *refs):
    factor_ref, a_high_ref, a_low_ref, *parts, stage_ref, panel_sem, part_sem = refs
    rows, width = mine_ref.shape
    arrivals = [
        fetch(mine_ref.at[:, cols], stage_ref.at[:, cols], panel_sem.at[at])
        for at, cols in enumerate(panels(width))
    ]
    cuts = row_cuts(mine_ref, parts, skip, part_sem)
    integral = jnp.zeros((rows, rows), jnp.float32)
    cross = jnp.zeros((rows, rows), jnp.float32)
    for copy, cols in zip(arrivals, panels(width)):
        copy.wait()
        high, low = halves(stage_ref[:, cols])
        factor_ref[:rows, cols] = high
        factor_ref[rows:, cols] = low
        integral += mxu(high, high, NT)
        cross += mxu(high, low, NT)
    integral = integral + (cross + cross.T)
    a_high, a_low = halves(integral / (gap_row_ref[...] + gap_col_ref[...]))
    a_high_ref[...] = a_high
    a_low_ref[...] = a_low
    for copy in cuts:
        copy.wait()


def step_kernel(plan, *refs):
    count, own, inner_rows = plan
    refs = list(refs)
    take = lambda number: [refs.pop(0) for _ in range(number)]
    others = take(count)
    factor_ref, gap_row_ref, gap_col_ref = take(3)
    begin = take(2 if own else 1)
    inner_ref = take(1)[0] if inner_rows else None
    gamma_ref, both_ref, stage_ref, in_sem, out_sem = take(5)
    rows, width = stage_ref.shape
    extent = both_ref.shape[0] // 2
    if inner_rows:
        inner_stage_ref, inner_sem = take(2)
        at, height = inner_rows
        inner_copy = fetch(inner_ref.at[pl.ds(at, height)], inner_stage_ref, inner_sem)
        others.append(inner_stage_ref)
    if not own:
        arrivals = [
            fetch(begin[0].at[:, cols], stage_ref.at[:, cols], in_sem.at[at])
            for at, cols in enumerate(panels(width))
        ]
    if inner_rows:
        inner_copy.wait()
    main = jnp.zeros((rows, 2 * extent), jnp.float32)
    rest = jnp.zeros((rows, extent), jnp.float32)
    for cols in panels(width):
        high, low = halves(jnp.concatenate([ref[:, cols] for ref in others], axis=0))
        both = jnp.concatenate([high, low], axis=0)
        both_ref[:, cols] = both
        main += mxu(factor_ref[:rows, cols], both, NT)
        rest += mxu(factor_ref[rows:, cols], high, NT)
    integral = main[:, :extent] + (main[:, extent:] + rest)
    a_high, a_low = halves(integral / (gap_row_ref[...] + gap_col_ref[...]))
    a_twice = jnp.concatenate([a_high, a_high], axis=1)
    departures = []
    for at, cols in enumerate(panels(width)):
        both = both_ref[:, cols]
        gamma = mxu(a_twice, both) + mxu(a_low, both[:extent])
        if own:
            high, low = factor_ref[:rows, cols], factor_ref[rows:, cols]
            a_high_own, a_low_own = begin[0][...], begin[1][...]
            gamma += mxu(a_high_own, high) + (mxu(a_high_own, low) + mxu(a_low_own, high))
        else:
            arrivals[at].wait()
            gamma += stage_ref[:, cols]
        stage_ref[:, cols] = gamma
        departures.append(fetch(stage_ref.at[:, cols], gamma_ref.at[:, cols], out_sem.at[at]))
    for copy in departures:
        copy.wait()


VMEM = pl.BlockSpec(memory_space=pltpu.VMEM)
HBM = pl.BlockSpec(memory_space=pltpu.HBM)


def cost(rows, extent, width):
    return pl.CostEstimate(flops=12 * rows * extent * width, bytes_accessed=4 * extent * width, transcendentals=0)


def in_vmem(array):
    return pltpu.with_memory_space_constraint(array, pltpu.VMEM)


def in_hbm(array):
    return pltpu.with_memory_space_constraint(array, pltpu.HBM)


def params(mebibytes):
    return pltpu.CompilerParams(vmem_limit_bytes=mebibytes << 20)


def cut_call(mine, count, height):
    width = mine.shape[1]
    return pl.pallas_call(
        functools.partial(cut_kernel, count),
        out_shape=(pltpu.HBM((height, width), jnp.float32),) * count,
        in_specs=[HBM],
        out_specs=(HBM,) * count,
        scratch_shapes=[pltpu.SemaphoreType.DMA((count,))],
        compiler_params=params(2),
        cost_estimate=pl.CostEstimate(flops=0, bytes_accessed=8 * count * height * width, transcendentals=0),
        name="first_cuts",
    )(in_hbm(mine))


def own_call(mine, gap_row, gap_col, skip, height):
    rows, width = mine.shape
    count = rows // height - skip
    factor = pltpu.VMEM((2 * rows, width), jnp.bfloat16)
    amplitude = pltpu.VMEM((rows, rows), jnp.bfloat16)
    part = pltpu.HBM((height, width), jnp.float32)
    return pl.pallas_call(
        functools.partial(own_kernel, skip),
        out_shape=(factor, amplitude, amplitude) + (part,) * count,
        in_specs=[HBM, VMEM, VMEM],
        out_specs=(VMEM,) * 3 + (HBM,) * count,
        scratch_shapes=[
            pltpu.VMEM((rows, width), jnp.float32),
            pltpu.SemaphoreType.DMA((width // PANEL,)),
            pltpu.SemaphoreType.DMA((count,)),
        ],
        compiler_params=params(10),
        cost_estimate=cost(rows, rows, width),
        name="own_block",
    )(in_hbm(mine), gap_row, gap_col)


def step_call(others, factor, gap_row, gap_col, begin, inner, inner_rows, name):
    rows, width = factor.shape[0] // 2, factor.shape[1]
    own = len(begin) == 2
    extent = sum(other.shape[0] for other in others)
    panel_sem = pltpu.SemaphoreType.DMA((width // PANEL,))
    scratch = [pltpu.VMEM((rows, width), jnp.float32), panel_sem, panel_sem]
    if inner_rows:
        extent += inner_rows[1]
        scratch += [pltpu.VMEM((inner_rows[1], width), jnp.float32), pltpu.SemaphoreType.DMA]
    begin = list(map(in_vmem if own else in_hbm, begin))
    extra = [in_hbm(inner)] if inner_rows else []
    return pl.pallas_call(
        functools.partial(step_kernel, (len(others), own, inner_rows)),
        out_shape=pltpu.HBM((rows, width), jnp.float32),
        in_specs=[VMEM] * (len(others) + 3) + [VMEM if own else HBM] * len(begin) + [HBM] * len(extra),
        out_specs=HBM,
        scratch_shapes=[pltpu.VMEM((2 * extent, width), jnp.bfloat16)] + scratch,
        compiler_params=params(12),
        cost_estimate=cost(rows, extent, width),
        name=name,
    )(*map(in_vmem, others), in_vmem(factor), gap_row, gap_col, *begin, *extra)


def local(b_factors, occ_energy, vir_energy):
    occ_block, vir_block, width = b_factors.shape
    occ_count = lax.axis_size("occ")
    vir_count = lax.axis_size("vir")
    occ_here = lax.axis_index("occ")
    vir_here = lax.axis_index("vir")

    def moved(block, target):
        route = []
        for occ in range(occ_count):
            for vir in range(vir_count):
                occ_to, vir_to = target(occ, vir)
                route.append(
                    (occ * vir_count + vir, occ_to % occ_count * vir_count + vir_to % vir_count)
                )
        return lax.ppermute(block, AXES, route)

    def across(occ, vir):
        return occ ^ 1, vir

    def along(occ, vir):
        return (occ - 2 if occ % 2 else occ + 2), vir

    def outward(occ, vir):
        return occ ^ 1, (vir + 1 if vir % 2 else vir - 1)

    def inward(occ, vir):
        return occ, vir ^ 1

    def gap_of(occ_place, vir_place):
        occ_part = lax.dynamic_slice_in_dim(
            occ_energy, occ_place % occ_count * occ_block, occ_block
        )
        vir_part = lax.dynamic_slice_in_dim(
            vir_energy, vir_place % vir_count * vir_block, vir_block
        )
        return occ_part[:, None] - vir_part[None, :]

    occ_side = 1 - 2 * (occ_here % 2)
    vir_side = 1 - 2 * (vir_here % 2)
    gap = gap_of(occ_here, vir_here)
    gap_inner = gap_of(occ_here, vir_here + vir_side)
    gap_near = gap_of(occ_here + occ_side, vir_here)
    gap_far = gap_of(occ_here + occ_count - occ_side, vir_here)
    gap_outer = gap_of(occ_here, vir_here + vir_count - vir_side)
    gap_row = gap.reshape(-1, 1)
    gap_step = jnp.concatenate([gap_near, gap_far, gap_outer], axis=1)
    gap_inner = gap_inner.reshape(1, -1)

    def held(value, *earlier):
        return lax.optimization_barrier((value, earlier))[0]

    mine = b_factors.reshape(occ_block * vir_block, width)
    parts = list(cut_call(mine, 2, vir_block))
    near = [moved(part, across) for part in parts]
    inner = moved(held(b_factors, *parts), inward).reshape(mine.shape)
    factor, a_high, a_low, *rest = own_call(held(mine, *parts), gap_row, gap.reshape(1, -1), 2, vir_block)
    parts += rest

    done = [a_high, a_high]
    far, outer = [], []
    begin = [a_high, a_low]
    inner_at = 0

    def step(k, *earlier):
        nonlocal begin, inner_at
        others = [near[k], far[k], outer[k]]
        if earlier:
            others = [held(other, *earlier) for other in others]
        gap_col = gap_step[k : k + 1]
        rows = None
        final = k == occ_block - 1
        if k >= FIRST_INNER and not final:
            height = mine.shape[0] // (occ_block - 1 - FIRST_INNER)
            rows = (inner_at, height)
            gap_col = jnp.concatenate([gap_col, gap_inner[:, inner_at : inner_at + height]], axis=1)
            inner_at += height
        gamma = step_call(others, factor, gap_row, gap_col, begin, inner, rows, "step_%d" % k)
        begin = [gamma]
        done.append(gamma)
        return gamma

    for k in range(occ_block):
        part = held(near[k], done[k])
        far.append(moved(part, along))
        outer.append(moved(part, outward))
        if k + 2 < occ_block:
            near.append(moved(held(parts[k + 2], part), across))
        if k > 0:
            step(k - 1, part)
    gamma = step(occ_block - 1)
    return gamma.reshape(occ_block, vir_block, width)


def solution(mesh):
    in_specs = (P("occ", "vir", None), P(), P())
    out_specs = P("occ", "vir", None)
    return jax.shard_map(local, mesh=mesh, in_specs=in_specs, out_specs=out_specs, check_vma=False)
```

```python
import functools
import jax
import jax.numpy as jnp
from jax import lax
from jax.experimental import pallas as pl
from jax.experimental.pallas import tpu as pltpu
from jax.sharding import PartitionSpec as P

AXES = ("occ", "vir")
PANEL = 512
NT = (((1,), (1,)), ((), ()))
NN = (((1,), (0,)), ((), ()))


def mxu(left, right, dims=NN):
    return lax.dot_general(left, right, dims, preferred_element_type=jnp.float32)


def halves(value):
    high = value.astype(jnp.bfloat16)
    low = (value - high.astype(jnp.float32)).astype(jnp.bfloat16)
    return high, low


def panels(width):
    return [slice(at, at + PANEL) for at in range(0, width, PANEL)]


def fetch(source_ref, target_ref, sem):
    copy = pltpu.make_async_copy(source_ref, target_ref, sem)
    copy.start()
    return copy


def row_cuts(mine_ref, targets, first, sem):
    height = targets[0].shape[0]
    copies = []
    for at, target in enumerate(targets):
        rows = pl.ds((first + at) * height, height)
        copies.append(fetch(mine_ref.at[rows], target, sem.at[at]))
    return copies


def cut_kernel(count, mine_ref, *refs):
    for copy in row_cuts(mine_ref, refs[:count], 0, refs[count]):
        copy.wait()


def own_kernel(skip, mine_ref, gap_row_ref, gap_col_ref, *refs):
    high_ref, low_ref, a_high_ref, a_low_ref, *parts, stage_ref, panel_sem, part_sem = refs
    rows, width = mine_ref.shape
    arrivals = [
        fetch(mine_ref.at[:, cols], stage_ref.at[:, cols], panel_sem.at[at])
        for at, cols in enumerate(panels(width))
    ]
    integral = jnp.zeros((rows, rows), jnp.float32)
    cross = jnp.zeros((rows, rows), jnp.float32)
    for copy, cols in zip(arrivals, panels(width)):
        copy.wait()
        high, low = halves(stage_ref[:, cols])
        high_ref[:, cols] = high
        low_ref[:, cols] = low
        integral += mxu(high, high, NT)
        cross += mxu(high, low, NT)
    cuts = row_cuts(stage_ref, parts, skip, part_sem)
    integral = integral + (cross + cross.T)
    a_high, a_low = halves(integral / (gap_row_ref[...] + gap_col_ref[...]))
    a_high_ref[...] = a_high
    a_low_ref[...] = a_low
    for copy in cuts:
        copy.wait()


def step_kernel(plan, *refs):
    count, own, inner_rows, final = plan
    refs = list(refs)
    take = lambda number: [refs.pop(0) for _ in range(number)]
    others = take(count)
    high_ref, low_ref, gap_row_ref, gap_col_ref = take(4)
    a_own = [ref[...] for ref in take(2)] if own else None
    start_ref = None if own else take(1)[0]
    inner_ref = take(1)[0] if inner_rows else None
    gamma_ref, both_ref = take(2)
    if inner_rows:
        inner_stage_ref, inner_sem = take(2)
        at, height = inner_rows
        fetch(inner_ref.at[pl.ds(at, height)], inner_stage_ref, inner_sem).wait()
        others.append(inner_stage_ref)
    rows, width = high_ref.shape
    extent = both_ref.shape[0] // 2
    main = jnp.zeros((rows, 2 * extent), jnp.float32)
    rest = jnp.zeros((rows, extent), jnp.float32)
    for cols in panels(width):
        high, low = halves(jnp.concatenate([ref[:, cols] for ref in others], axis=0))
        both = jnp.concatenate([high, low], axis=0)
        both_ref[:, cols] = both
        main += mxu(high_ref[:, cols], both, NT)
        rest += mxu(low_ref[:, cols], high, NT)
    integral = main[:, :extent] + (main[:, extent:] + rest)
    a_high, a_low = halves(integral / (gap_row_ref[...] + gap_col_ref[...]))
    a_twice = jnp.concatenate([a_high, a_high], axis=1)
    departures = []
    for at, cols in enumerate(panels(width)):
        both = both_ref[:, cols]
        gamma = mxu(a_twice, both) + mxu(a_low, both[:extent])
        if own:
            high, low = high_ref[:, cols], low_ref[:, cols]
            gamma += mxu(a_own[0], high) + (mxu(a_own[0], low) + mxu(a_own[1], high))
        else:
            gamma += start_ref[:, cols]
        if final:
            stage_ref, sem = refs
            stage_ref[:, cols] = gamma
            departures.append(fetch(stage_ref.at[:, cols], gamma_ref.at[:, cols], sem.at[at]))
        else:
            gamma_ref[:, cols] = gamma
    for copy in departures:
        copy.wait()


VMEM = pl.BlockSpec(memory_space=pltpu.VMEM)
HBM = pl.BlockSpec(memory_space=pltpu.HBM)


def cost(rows, extent, width):
    return pl.CostEstimate(flops=12 * rows * extent * width, bytes_accessed=4 * extent * width, transcendentals=0)


def in_vmem(array):
    return pltpu.with_memory_space_constraint(array, pltpu.VMEM)


def in_hbm(array):
    return pltpu.with_memory_space_constraint(array, pltpu.HBM)


def params(mebibytes):
    return pltpu.CompilerParams(vmem_limit_bytes=mebibytes << 20)


def cut_call(mine, count, height):
    width = mine.shape[1]
    return pl.pallas_call(
        functools.partial(cut_kernel, count),
        out_shape=(pltpu.VMEM((height, width), jnp.float32),) * count,
        in_specs=[HBM],
        out_specs=(VMEM,) * count,
        scratch_shapes=[pltpu.SemaphoreType.DMA((count,))],
        compiler_params=params(2),
        cost_estimate=pl.CostEstimate(flops=0, bytes_accessed=8 * count * height * width, transcendentals=0),
        name="first_cuts",
    )(in_hbm(mine))


def own_call(mine, gap_row, gap_col, skip, height):
    rows, width = mine.shape
    count = rows // height - skip
    factor = pltpu.VMEM((rows, width), jnp.bfloat16)
    amplitude = pltpu.VMEM((rows, rows), jnp.bfloat16)
    part = pltpu.HBM((height, width), jnp.float32)
    return pl.pallas_call(
        functools.partial(own_kernel, skip),
        out_shape=(factor, factor, amplitude, amplitude) + (part,) * count,
        in_specs=[HBM, VMEM, VMEM],
        out_specs=(VMEM,) * 4 + (HBM,) * count,
        scratch_shapes=[
            pltpu.VMEM((rows, width), jnp.float32),
            pltpu.SemaphoreType.DMA((width // PANEL,)),
            pltpu.SemaphoreType.DMA((count,)),
        ],
        compiler_params=params(10),
        cost_estimate=cost(rows, rows, width),
        name="own_block",
    )(in_hbm(mine), gap_row, gap_col)


def step_call(others, high, low, gap_row, gap_col, begin, inner, inner_rows, final, name):
    rows, width = high.shape
    own = len(begin) == 2
    extent = sum(other.shape[0] for other in others)
    scratch = []
    if inner_rows:
        extent += inner_rows[1]
        scratch += [pltpu.VMEM((inner_rows[1], width), jnp.float32), pltpu.SemaphoreType.DMA]
    if final:
        scratch += [pltpu.VMEM((rows, width), jnp.float32), pltpu.SemaphoreType.DMA((width // PANEL,))]
    extra = [in_hbm(inner)] if inner_rows else []
    return pl.pallas_call(
        functools.partial(step_kernel, (len(others), own, inner_rows, final)),
        out_shape=(pltpu.HBM if final else pltpu.VMEM)((rows, width), jnp.float32),
        in_specs=[VMEM] * (len(others) + 4 + len(begin)) + [HBM] * len(extra),
        out_specs=HBM if final else VMEM,
        scratch_shapes=[pltpu.VMEM((2 * extent, width), jnp.bfloat16)] + scratch,
        input_output_aliases={} if final or own else {len(others) + 4: 0},
        compiler_params=params(10),
        cost_estimate=cost(rows, extent, width),
        name=name,
    )(*map(in_vmem, others), in_vmem(high), in_vmem(low), gap_row, gap_col, *map(in_vmem, begin), *extra)


def local(b_factors, occ_energy, vir_energy):
    occ_block, vir_block, width = b_factors.shape
    occ_count = lax.axis_size("occ")
    vir_count = lax.axis_size("vir")
    occ_here = lax.axis_index("occ")
    vir_here = lax.axis_index("vir")

    def moved(block, target):
        route = []
        for occ in range(occ_count):
            for vir in range(vir_count):
                occ_to, vir_to = target(occ, vir)
                route.append(
                    (occ * vir_count + vir, occ_to % occ_count * vir_count + vir_to % vir_count)
                )
        return lax.ppermute(block, AXES, route)

    def across(occ, vir):
        return occ ^ 1, vir

    def along(occ, vir):
        return (occ - 2 if occ % 2 else occ + 2), vir

    def outward(occ, vir):
        return occ ^ 1, (vir + 1 if vir % 2 else vir - 1)

    def inward(occ, vir):
        return occ, vir ^ 1

    def gap_of(occ_place, vir_place):
        occ_part = lax.dynamic_slice_in_dim(
            occ_energy, occ_place % occ_count * occ_block, occ_block
        )
        vir_part = lax.dynamic_slice_in_dim(
            vir_energy, vir_place % vir_count * vir_block, vir_block
        )
        return occ_part[:, None] - vir_part[None, :]

    occ_side = 1 - 2 * (occ_here % 2)
    vir_side = 1 - 2 * (vir_here % 2)
    gap = gap_of(occ_here, vir_here)
    gap_inner = gap_of(occ_here, vir_here + vir_side)
    gap_near = gap_of(occ_here + occ_side, vir_here)
    gap_far = gap_of(occ_here + occ_count - occ_side, vir_here)
    gap_outer = gap_of(occ_here, vir_here + vir_count - vir_side)
    gap_row = gap.reshape(-1, 1)
    gap_step = jnp.concatenate([gap_near, gap_far, gap_outer], axis=1)
    gap_inner = gap_inner.reshape(1, -1)

    def held(value, *earlier):
        return lax.optimization_barrier((value, earlier))[0]

    mine = b_factors.reshape(occ_block * vir_block, width)
    parts = list(cut_call(mine, 2, vir_block))
    near = [moved(part, across) for part in parts]
    inner = moved(held(b_factors, *parts), inward).reshape(mine.shape)
    high, low, a_high, a_low, *rest = own_call(held(mine, *parts), gap_row, gap.reshape(1, -1), 2, vir_block)
    parts += rest

    done = [a_high, a_high]
    far, outer = [], []
    begin = [a_high, a_low]
    inner_at = 0

    def step(k, *earlier):
        nonlocal begin, inner_at
        others = [near[k], far[k], outer[k]]
        if earlier:
            others = [held(other, *earlier) for other in others]
        gap_col = gap_step[k : k + 1]
        rows = None
        final = k == occ_block - 1
        if not final:
            height = vir_block if k < occ_block - 2 else 2 * vir_block
            rows = (inner_at, height)
            gap_col = jnp.concatenate([gap_col, gap_inner[:, inner_at : inner_at + height]], axis=1)
            inner_at += height
        gamma = step_call(others, high, low, gap_row, gap_col, begin, inner, rows, final, "step_%d" % k)
        begin = [gamma]
        done.append(gamma)
        return gamma

    for k in range(occ_block):
        part = held(near[k], done[k], inner) if k == 1 else held(near[k], done[k])
        far.append(moved(part, along))
        outer.append(moved(part, outward))
        if k + 2 < occ_block:
            near.append(moved(held(parts[k + 2], part), across))
        if k > 0:
            step(k - 1, part)
    gamma = step(occ_block - 1)
    return gamma.reshape(occ_block, vir_block, width)


def solution(mesh):
    in_specs = (P("occ", "vir", None), P(), P())
    out_specs = P("occ", "vir", None)
    return jax.shard_map(local, mesh=mesh, in_specs=in_specs, out_specs=out_specs, check_vma=False)
```

```python
import functools
import jax
import jax.numpy as jnp
from jax import lax
from jax.experimental import pallas as pl
from jax.experimental.pallas import tpu as pltpu
from jax.sharding import PartitionSpec as P

AXES = ("occ", "vir")
PANEL = 512
NT = (((1,), (1,)), ((), ()))
NN = (((1,), (0,)), ((), ()))


def mxu(left, right, dims=NN):
    return lax.dot_general(left, right, dims, preferred_element_type=jnp.float32)


def halves(value):
    high = value.astype(jnp.bfloat16)
    low = (value - high.astype(jnp.float32)).astype(jnp.bfloat16)
    return high, low


def panels(width):
    return [slice(at, at + PANEL) for at in range(0, width, PANEL)]


def fetch(source_ref, target_ref, sem):
    copy = pltpu.make_async_copy(source_ref, target_ref, sem)
    copy.start()
    return copy


def row_cuts(mine_ref, targets, first, sem):
    height = targets[0].shape[0]
    copies = []
    for at, target in enumerate(targets):
        rows = pl.ds((first + at) * height, height)
        copies.append(fetch(mine_ref.at[rows], target, sem.at[at]))
    return copies


def cut_kernel(count, mine_ref, *refs):
    for copy in row_cuts(mine_ref, refs[:count], 0, refs[count]):
        copy.wait()


def own_kernel(skip, mine_ref, gap_row_ref, gap_col_ref, *refs):
    high_ref, low_ref, a_high_ref, a_low_ref, *parts, stage_ref, panel_sem, part_sem = refs
    rows, width = mine_ref.shape
    arrivals = [
        fetch(mine_ref.at[:, cols], stage_ref.at[:, cols], panel_sem.at[at])
        for at, cols in enumerate(panels(width))
    ]
    integral = jnp.zeros((rows, rows), jnp.float32)
    cross = jnp.zeros((rows, rows), jnp.float32)
    for copy, cols in zip(arrivals, panels(width)):
        copy.wait()
        high, low = halves(stage_ref[:, cols])
        high_ref[:, cols] = high
        low_ref[:, cols] = low
        integral += mxu(high, high, NT)
        cross += mxu(high, low, NT)
    cuts = row_cuts(stage_ref, parts, skip, part_sem)
    integral = integral + (cross + cross.T)
    a_high, a_low = halves(integral / (gap_row_ref[...] + gap_col_ref[...]))
    a_high_ref[...] = a_high
    a_low_ref[...] = a_low
    for copy in cuts:
        copy.wait()


def step_kernel(plan, *refs):
    count, own, inner_rows, final = plan
    refs = list(refs)
    take = lambda number: [refs.pop(0) for _ in range(number)]
    others = take(count)
    high_ref, low_ref, gap_row_ref, gap_col_ref = take(4)
    a_own = [ref[...] for ref in take(2)] if own else None
    start_ref = None if own else take(1)[0]
    inner_ref = take(1)[0] if inner_rows else None
    gamma_ref, both_ref = take(2)
    if inner_rows:
        inner_stage_ref, inner_sem = take(2)
        at, height = inner_rows
        fetch(inner_ref.at[pl.ds(at, height)], inner_stage_ref, inner_sem).wait()
        others.append(inner_stage_ref)
    rows, width = high_ref.shape
    extent = both_ref.shape[0] // 2
    main = jnp.zeros((rows, 2 * extent), jnp.float32)
    rest = jnp.zeros((rows, extent), jnp.float32)
    for cols in panels(width):
        high, low = halves(jnp.concatenate([ref[:, cols] for ref in others], axis=0))
        both = jnp.concatenate([high, low], axis=0)
        both_ref[:, cols] = both
        main += mxu(high_ref[:, cols], both, NT)
        rest += mxu(low_ref[:, cols], high, NT)
    integral = main[:, :extent] + (main[:, extent:] + rest)
    a_high, a_low = halves(integral / (gap_row_ref[...] + gap_col_ref[...]))
    a_twice = jnp.concatenate([a_high, a_high], axis=1)
    departures = []
    for at, cols in enumerate(panels(width)):
        both = both_ref[:, cols]
        gamma = mxu(a_twice, both) + mxu(a_low, both[:extent])
        if own:
            high, low = high_ref[:, cols], low_ref[:, cols]
            gamma += mxu(a_own[0], high) + (mxu(a_own[0], low) + mxu(a_own[1], high))
        else:
            gamma += start_ref[:, cols]
        if final:
            stage_ref, sem = refs
            stage_ref[:, cols] = gamma
            departures.append(fetch(stage_ref.at[:, cols], gamma_ref.at[:, cols], sem.at[at]))
        else:
            gamma_ref[:, cols] = gamma
    for copy in departures:
        copy.wait()


VMEM = pl.BlockSpec(memory_space=pltpu.VMEM)
HBM = pl.BlockSpec(memory_space=pltpu.HBM)


def cost(rows, extent, width):
    return pl.CostEstimate(flops=12 * rows * extent * width, bytes_accessed=4 * extent * width, transcendentals=0)


def in_vmem(array):
    return pltpu.with_memory_space_constraint(array, pltpu.VMEM)


def in_hbm(array):
    return pltpu.with_memory_space_constraint(array, pltpu.HBM)


def params(mebibytes):
    return pltpu.CompilerParams(vmem_limit_bytes=mebibytes << 20)


def cut_call(mine, count, height):
    width = mine.shape[1]
    return pl.pallas_call(
        functools.partial(cut_kernel, count),
        out_shape=(pltpu.VMEM((height, width), jnp.float32),) * count,
        in_specs=[HBM],
        out_specs=(VMEM,) * count,
        scratch_shapes=[pltpu.SemaphoreType.DMA((count,))],
        compiler_params=params(2),
        cost_estimate=pl.CostEstimate(flops=0, bytes_accessed=8 * count * height * width, transcendentals=0),
        name="first_cuts",
    )(in_hbm(mine))


def own_call(mine, gap_row, gap_col, skip, height):
    rows, width = mine.shape
    count = rows // height - skip
    factor = pltpu.VMEM((rows, width), jnp.bfloat16)
    amplitude = pltpu.VMEM((rows, rows), jnp.bfloat16)
    part = pltpu.HBM((height, width), jnp.float32)
    return pl.pallas_call(
        functools.partial(own_kernel, skip),
        out_shape=(factor, factor, amplitude, amplitude) + (part,) * count,
        in_specs=[HBM, VMEM, VMEM],
        out_specs=(VMEM,) * 4 + (HBM,) * count,
        scratch_shapes=[
            pltpu.VMEM((rows, width), jnp.float32),
            pltpu.SemaphoreType.DMA((width // PANEL,)),
            pltpu.SemaphoreType.DMA((count,)),
        ],
        compiler_params=params(10),
        cost_estimate=cost(rows, rows, width),
        name="own_block",
    )(in_hbm(mine), gap_row, gap_col)


def step_call(others, high, low, gap_row, gap_col, begin, inner, inner_rows, final, name):
    rows, width = high.shape
    own = len(begin) == 2
    extent = sum(other.shape[0] for other in others)
    scratch = []
    if inner_rows:
        extent += inner_rows[1]
        scratch += [pltpu.VMEM((inner_rows[1], width), jnp.float32), pltpu.SemaphoreType.DMA]
    if final:
        scratch += [pltpu.VMEM((rows, width), jnp.float32), pltpu.SemaphoreType.DMA((width // PANEL,))]
    extra = [in_hbm(inner)] if inner_rows else []
    return pl.pallas_call(
        functools.partial(step_kernel, (len(others), own, inner_rows, final)),
        out_shape=(pltpu.HBM if final else pltpu.VMEM)((rows, width), jnp.float32),
        in_specs=[VMEM] * (len(others) + 4 + len(begin)) + [HBM] * len(extra),
        out_specs=HBM if final else VMEM,
        scratch_shapes=[pltpu.VMEM((2 * extent, width), jnp.bfloat16)] + scratch,
        input_output_aliases={} if final or own else {len(others) + 4: 0},
        compiler_params=params(10),
        cost_estimate=cost(rows, extent, width),
        name=name,
    )(*map(in_vmem, others), in_vmem(high), in_vmem(low), gap_row, gap_col, *map(in_vmem, begin), *extra)


def local(b_factors, occ_energy, vir_energy):
    occ_block, vir_block, width = b_factors.shape
    occ_count = lax.axis_size("occ")
    vir_count = lax.axis_size("vir")
    occ_here = lax.axis_index("occ")
    vir_here = lax.axis_index("vir")

    def moved(block, target):
        route = []
        for occ in range(occ_count):
            for vir in range(vir_count):
                occ_to, vir_to = target(occ, vir)
                route.append(
                    (occ * vir_count + vir, occ_to % occ_count * vir_count + vir_to % vir_count)
                )
        return lax.ppermute(block, AXES, route)

    def across(occ, vir):
        return occ ^ 1, vir

    def along(occ, vir):
        return (occ - 2 if occ % 2 else occ + 2), vir

    def outward(occ, vir):
        return occ ^ 1, (vir + 1 if vir % 2 else vir - 1)

    def inward(occ, vir):
        return occ, vir ^ 1

    def gap_of(occ_place, vir_place):
        occ_part = lax.dynamic_slice_in_dim(
            occ_energy, occ_place % occ_count * occ_block, occ_block
        )
        vir_part = lax.dynamic_slice_in_dim(
            vir_energy, vir_place % vir_count * vir_block, vir_block
        )
        return occ_part[:, None] - vir_part[None, :]

    occ_side = 1 - 2 * (occ_here % 2)
    vir_side = 1 - 2 * (vir_here % 2)
    gap = gap_of(occ_here, vir_here)
    gap_inner = gap_of(occ_here, vir_here + vir_side)
    gap_near = gap_of(occ_here + occ_side, vir_here)
    gap_far = gap_of(occ_here + occ_count - occ_side, vir_here)
    gap_outer = gap_of(occ_here, vir_here + vir_count - vir_side)
    gap_row = gap.reshape(-1, 1)
    gap_step = jnp.concatenate([gap_near, gap_far, gap_outer], axis=1)
    gap_inner = gap_inner.reshape(1, -1)

    def held(value, *earlier):
        return lax.optimization_barrier((value, earlier))[0]

    mine = b_factors.reshape(occ_block * vir_block, width)
    parts = list(cut_call(mine, 1, vir_block))
    near = [moved(part, across) for part in parts]
    high, low, a_high, a_low, *rest = own_call(held(mine, *parts), gap_row, gap.reshape(1, -1), 1, vir_block)
    parts += rest
    near.append(moved(parts[1], across))
    inner = moved(held(b_factors, parts[0]), inward).reshape(mine.shape)

    done = [a_high, a_high]
    far, outer = [], []
    begin = [a_high, a_low]
    inner_at = 0

    def step(k, *earlier):
        nonlocal begin, inner_at
        others = [near[k], far[k], outer[k]]
        if earlier:
            others = [held(other, *earlier) for other in others]
        gap_col = gap_step[k : k + 1]
        rows = None
        final = k == occ_block - 1
        if not final:
            height = vir_block if k < occ_block - 2 else 2 * vir_block
            rows = (inner_at, height)
            gap_col = jnp.concatenate([gap_col, gap_inner[:, inner_at : inner_at + height]], axis=1)
            inner_at += height
        gamma = step_call(others, high, low, gap_row, gap_col, begin, inner, rows, final, "step_%d" % k)
        begin = [gamma]
        done.append(gamma)
        return gamma

    for k in range(occ_block):
        part = held(near[k], done[k], inner) if k == 1 else held(near[k], done[k])
        far.append(moved(part, along))
        outer.append(moved(part, outward))
        if k + 2 < occ_block:
            near.append(moved(held(parts[k + 2], part), across))
        if k > 0:
            step(k - 1, part)
    gamma = step(occ_block - 1)
    return gamma.reshape(occ_block, vir_block, width)


def solution(mesh):
    in_specs = (P("occ", "vir", None), P(), P())
    out_specs = P("occ", "vir", None)
    return jax.shard_map(local, mesh=mesh, in_specs=in_specs, out_specs=out_specs, check_vma=False)
```

```python
import functools
import jax
import jax.numpy as jnp
from jax import lax
from jax.experimental import pallas as pl
from jax.experimental.pallas import tpu as pltpu
from jax.sharding import PartitionSpec as P

AXES = ("occ", "vir")
PANEL = 1024
NT = (((1,), (1,)), ((), ()))
NN = (((1,), (0,)), ((), ()))


def mxu(left, right, dims=NN):
    return lax.dot_general(left, right, dims, preferred_element_type=jnp.float32)


def halves(value):
    high = value.astype(jnp.bfloat16)
    low = (value - high.astype(jnp.float32)).astype(jnp.bfloat16)
    return high, low


def panels(width):
    return [slice(at, at + PANEL) for at in range(0, width, PANEL)]


def fetch(source_ref, target_ref, sem):
    copy = pltpu.make_async_copy(source_ref, target_ref, sem)
    copy.start()
    return copy


def row_cuts(mine_ref, targets, starts, sem):
    copies = []
    for at, (target, start) in enumerate(zip(targets, starts)):
        rows = pl.ds(start, target.shape[0])
        copies.append(fetch(mine_ref.at[rows], target, sem.at[at]))
    return copies


def cut_kernel(starts, mine_ref, *refs):
    for copy in row_cuts(mine_ref, refs[:-1], starts, refs[-1]):
        copy.wait()


def over_panels(width, body, start):
    def turn(at, state):
        return body(at, pl.ds(pl.multiple_of(at * PANEL, PANEL), PANEL), state)

    return lax.fori_loop(0, width // PANEL, turn, start)


def own_kernel(starts, mine_ref, gap_row_ref, gap_col_ref, *refs):
    high_ref, low_ref, a_high_ref, a_low_ref, *parts, stage_ref, panel_sem, part_sem = refs
    rows, width = mine_ref.shape
    for at, cols in enumerate(panels(width)):
        fetch(mine_ref.at[:, cols], stage_ref.at[:, cols], panel_sem.at[at])

    def body(at, cols, state):
        integral, cross = state
        pltpu.make_async_copy(mine_ref.at[:, cols], stage_ref.at[:, cols], panel_sem.at[at]).wait()
        high, low = halves(stage_ref[:, cols])
        high_ref[:, cols] = high
        low_ref[:, cols] = low
        return integral + mxu(high, high, NT), cross + mxu(high, low, NT)

    zero = jnp.zeros((rows, rows), jnp.float32)
    integral, cross = over_panels(width, body, (zero, zero))
    cuts = row_cuts(stage_ref, parts, starts, part_sem)
    integral = integral + (cross + cross.T)
    a_high, a_low = halves(integral / (gap_row_ref[...] + gap_col_ref[...]))
    a_high_ref[...] = a_high
    a_low_ref[...] = a_low
    for copy in cuts:
        copy.wait()


def step_kernel(plan, *refs):
    count, own, inner_rows, gaps, final = plan
    refs = list(refs)
    take = lambda number: [refs.pop(0) for _ in range(number)]
    others = take(count)
    high_ref, low_ref, gap_row_ref, table_ref = take(4)
    a_own = take(2) if own else None
    start_ref = None if own else take(1)[0]
    inner_ref = take(1)[0] if inner_rows else None
    gamma_ref, both_ref = take(2)
    if inner_rows:
        inner_stage_ref, inner_sem = take(2)
        at, height = inner_rows
        fetch(inner_ref.at[pl.ds(at, height)], inner_stage_ref, inner_sem).wait()
        others.append(inner_stage_ref)
    rows, width = high_ref.shape
    extent = both_ref.shape[0] // 2

    def gather(at, cols, state):
        main, rest = state
        high, low = halves(jnp.concatenate([ref[:, cols] for ref in others], axis=0))
        both = jnp.concatenate([high, low], axis=0)
        both_ref[:, cols] = both
        return main + mxu(high_ref[:, cols], both, NT), rest + mxu(low_ref[:, cols], high, NT)

    start = (jnp.zeros((rows, 2 * extent), jnp.float32), jnp.zeros((rows, extent), jnp.float32))
    main, rest = over_panels(width, gather, start)
    integral = main[:, :extent] + (main[:, extent:] + rest)
    gap_col = jnp.concatenate(
        [table_ref[row : row + 1, at : at + height] for row, at, height in gaps], axis=1
    )
    a_high, a_low = halves(integral / (gap_row_ref[...] + gap_col))
    a_twice = jnp.concatenate([a_high, a_high], axis=1)

    def spread(at, cols, state):
        both = both_ref[:, cols]
        gamma = mxu(a_twice, both) + mxu(a_low, both[:extent])
        if own:
            high, low = high_ref[:, cols], low_ref[:, cols]
            a_high_own, a_low_own = a_own[0][...], a_own[1][...]
            gamma += mxu(a_high_own, high) + (mxu(a_high_own, low) + mxu(a_low_own, high))
        else:
            gamma += start_ref[:, cols]
        if final:
            stage_ref, sem = refs
            stage_ref[:, cols] = gamma
            fetch(stage_ref.at[:, cols], gamma_ref.at[:, cols], sem.at[at])
        else:
            gamma_ref[:, cols] = gamma
        return state

    over_panels(width, spread, 0)
    if final:
        stage_ref, sem = refs
        for at, cols in enumerate(panels(width)):
            pltpu.make_async_copy(stage_ref.at[:, cols], gamma_ref.at[:, cols], sem.at[at]).wait()


VMEM = pl.BlockSpec(memory_space=pltpu.VMEM)
HBM = pl.BlockSpec(memory_space=pltpu.HBM)


def cost(rows, extent, width):
    return pl.CostEstimate(flops=12 * rows * extent * width, bytes_accessed=4 * extent * width, transcendentals=0)


def in_vmem(array):
    return pltpu.with_memory_space_constraint(array, pltpu.VMEM)


def in_hbm(array):
    return pltpu.with_memory_space_constraint(array, pltpu.HBM)


def params(mebibytes):
    return pltpu.CompilerParams(vmem_limit_bytes=mebibytes << 20)


def cut_call(mine, ranges):
    width = mine.shape[1]
    count = len(ranges)
    return pl.pallas_call(
        functools.partial(cut_kernel, [start for start, _ in ranges]),
        out_shape=tuple(pltpu.VMEM((height, width), jnp.float32) for _, height in ranges),
        in_specs=[HBM],
        out_specs=(VMEM,) * count,
        scratch_shapes=[pltpu.SemaphoreType.DMA((count,))],
        compiler_params=params(2),
        cost_estimate=pl.CostEstimate(flops=0, bytes_accessed=1 << 20, transcendentals=0),
        name="first_cuts",
    )(in_hbm(mine))


def own_call(mine, gap_row, gap_col, ranges):
    rows, width = mine.shape
    count = len(ranges)
    factor = pltpu.VMEM((rows, width), jnp.bfloat16)
    amplitude = pltpu.VMEM((rows, rows), jnp.bfloat16)
    return pl.pallas_call(
        functools.partial(own_kernel, [start for start, _ in ranges]),
        out_shape=(factor, factor, amplitude, amplitude)
        + tuple(pltpu.HBM((height, width), jnp.float32) for _, height in ranges),
        in_specs=[HBM, VMEM, VMEM],
        out_specs=(VMEM,) * 4 + (HBM,) * count,
        scratch_shapes=[
            pltpu.VMEM((rows, width), jnp.float32),
            pltpu.SemaphoreType.DMA((width // PANEL,)),
            pltpu.SemaphoreType.DMA((count,)),
        ],
        compiler_params=params(10),
        cost_estimate=cost(rows, rows, width),
        name="own_block",
    )(in_hbm(mine), gap_row, gap_col)


def step_call(others, high, low, gap_row, table, gaps, begin, inner, inner_rows, final, name):
    rows, width = high.shape
    own = len(begin) == 2
    extent = sum(other.shape[0] for other in others)
    scratch = []
    if inner_rows:
        extent += inner_rows[1]
        scratch += [pltpu.VMEM((inner_rows[1], width), jnp.float32), pltpu.SemaphoreType.DMA]
    if final:
        scratch += [pltpu.VMEM((rows, width), jnp.float32), pltpu.SemaphoreType.DMA((width // PANEL,))]
    extra = [in_hbm(inner)] if inner_rows else []
    return pl.pallas_call(
        functools.partial(step_kernel, (len(others), own, inner_rows, gaps, final)),
        out_shape=(pltpu.HBM if final else pltpu.VMEM)((rows, width), jnp.float32),
        in_specs=[VMEM] * (len(others) + 4 + len(begin)) + [HBM] * len(extra),
        out_specs=HBM if final else VMEM,
        scratch_shapes=[pltpu.VMEM((2 * extent, width), jnp.bfloat16)] + scratch,
        input_output_aliases={} if final or own else {len(others) + 4: 0},
        compiler_params=params(10),
        cost_estimate=pl.CostEstimate(flops=1 << 20, bytes_accessed=1 << 16, transcendentals=0),
        name=name,
    )(*map(in_vmem, others), in_vmem(high), in_vmem(low), gap_row, table, *map(in_vmem, begin), *extra)


def local(b_factors, occ_energy, vir_energy):
    occ_block, vir_block, width = b_factors.shape
    occ_count = lax.axis_size("occ")
    vir_count = lax.axis_size("vir")
    occ_here = lax.axis_index("occ")
    vir_here = lax.axis_index("vir")

    def moved(block, target):
        route = []
        for occ in range(occ_count):
            for vir in range(vir_count):
                occ_to, vir_to = target(occ, vir)
                route.append(
                    (occ * vir_count + vir, occ_to % occ_count * vir_count + vir_to % vir_count)
                )
        return lax.ppermute(block, AXES, route)

    def across(occ, vir):
        return occ ^ 1, vir

    def back(occ, vir):
        return (occ + 2 if occ % 2 else occ - 2), vir

    def along(occ, vir):
        return (occ - 2 if occ % 2 else occ + 2), vir

    def outward(occ, vir):
        return occ ^ 1, (vir + 1 if vir % 2 else vir - 1)

    def inward(occ, vir):
        return occ, vir ^ 1

    def gap_of(occ_place, vir_place):
        occ_part = lax.dynamic_slice_in_dim(
            occ_energy, occ_place % occ_count * occ_block, occ_block
        )
        vir_part = lax.dynamic_slice_in_dim(
            vir_energy, vir_place % vir_count * vir_block, vir_block
        )
        return occ_part[:, None] - vir_part[None, :]

    occ_side = 1 - 2 * (occ_here % 2)
    vir_side = 1 - 2 * (vir_here % 2)
    gap = gap_of(occ_here, vir_here)
    gap_inner = gap_of(occ_here, vir_here + vir_side)
    gap_near = gap_of(occ_here + occ_side, vir_here)
    gap_far = gap_of(occ_here + occ_count - occ_side, vir_here)
    gap_outer = gap_of(occ_here, vir_here + vir_count - vir_side)
    gap_row = gap.reshape(-1, 1)
    table = jnp.concatenate([gap_near, gap_far, gap_outer, gap_inner], axis=1)

    def held(value, *earlier):
        return lax.optimization_barrier((value, earlier))[0]

    mine = b_factors.reshape(occ_block * vir_block, width)
    size = mine.shape[0]
    early = vir_block // 2
    count = occ_block
    ranges = [(k * vir_block, vir_block) for k in range(count)]

    first, ahead = cut_call(mine, [ranges[0], (size - early, early)])
    parts = [first]
    near = [moved(first, across)]
    inner = moved(held(b_factors, first), inward).reshape(size, width)
    ahead_back, ahead_out = moved(ahead, back), moved(ahead, outward)
    high, low, a_high, a_low, *rest = own_call(held(mine, first), gap_row, gap.reshape(1, -1), ranges[1:])
    parts += rest
    near.append(moved(held(parts[1], ahead_back, ahead_out), across))

    done = [a_high, a_high]
    far, outer = [], []
    begin = [a_high, a_low]
    inner_at = 0

    def step(k, *earlier):
        nonlocal begin, inner_at
        final = k == count - 1
        others = [near[k], far[k], outer[k]]
        rows = None
        if final:
            others.append(late)
            at = vir_block - early
            gaps = [(k, 0, vir_block)]
            gaps += [(k, which * vir_block + shift, early) for shift in (0, at) for which in (1, 2)]
        else:
            others = [held(other, *earlier) for other in others]
            height = vir_block if k < count - 2 else size - inner_at
            rows = (inner_at, height)
            gaps = [(k, 0, 3 * vir_block)]
            gaps += [(row, 3 * vir_block, vir_block) for row in range(inner_at // vir_block, (inner_at + height) // vir_block)]
            inner_at += height
        gamma = step_call(others, high, low, gap_row, table, gaps, begin, inner, rows, final, "step_%d" % k)
        begin = [gamma]
        done.append(gamma)
        return gamma

    late = None
    for k in range(count):
        part = held(near[k], done[k])
        if k == 0:
            part = held(part, inner)
        if k == count - 1:
            part = part[: vir_block - early]
        far.append(moved(part, along))
        outer.append(moved(part, outward))
        if k + 2 < count:
            near.append(moved(held(parts[k + 2], part), across))
        elif k + 2 == count:
            relayed = held(jnp.concatenate([ahead_back, ahead_out], axis=0), part, far[k - 1], outer[k - 1])
            late = moved(relayed, across)
        if k > 0:
            step(k - 1, part)
    gamma = step(count - 1)
    return gamma.reshape(occ_block, vir_block, width)


def solution(mesh):
    in_specs = (P("occ", "vir", None), P(), P())
    out_specs = P("occ", "vir", None)
    return jax.shard_map(local, mesh=mesh, in_specs=in_specs, out_specs=out_specs, check_vma=False)
```

```python
import functools
import jax
import jax.numpy as jnp
from jax import lax
from jax.experimental import pallas as pl
from jax.experimental.pallas import tpu as pltpu
from jax.sharding import PartitionSpec as P

AXES = ("occ", "vir")
PANEL = 1024
INNER_ROWS = (1, 1, 1, 1, 2, 2, 0)
NT = (((1,), (1,)), ((), ()))
NN = (((1,), (0,)), ((), ()))


def mxu(left, right, dims=NN):
    return lax.dot_general(left, right, dims, preferred_element_type=jnp.float32)


def halves(value):
    high = value.astype(jnp.bfloat16)
    low = (value - high.astype(jnp.float32)).astype(jnp.bfloat16)
    return high, low


def panels(width):
    return [slice(at, at + PANEL) for at in range(0, width, PANEL)]


def fetch(source_ref, target_ref, sem):
    copy = pltpu.make_async_copy(source_ref, target_ref, sem)
    copy.start()
    return copy


def row_cuts(mine_ref, targets, starts, sem):
    copies = []
    for at, (target, start) in enumerate(zip(targets, starts)):
        rows = pl.ds(start, target.shape[0])
        copies.append(fetch(mine_ref.at[rows], target, sem.at[at]))
    return copies


def cut_kernel(starts, mine_ref, *refs):
    for copy in row_cuts(mine_ref, refs[:-1], starts, refs[-1]):
        copy.wait()


def over_panels(width, body, start, unroll=2):
    def turn(at, state):
        return body(at, pl.ds(pl.multiple_of(at * PANEL, PANEL), PANEL), state)

    return lax.fori_loop(0, width // PANEL, turn, start, unroll=unroll)


def split_kernel(starts, mine_ref, *refs):
    *parts, stage_ref, in_sem, out_sem = refs
    arrivals, departures = [], []
    for at, (part, start) in enumerate(zip(parts, starts)):
        rows = pl.ds(start, part.shape[0])
        arrivals.append(fetch(mine_ref.at[rows], stage_ref.at[rows], in_sem.at[at]))
    for at, (part, start) in enumerate(zip(parts, starts)):
        arrivals[at].wait()
        departures.append(fetch(stage_ref.at[pl.ds(start, part.shape[0])], part, out_sem.at[at]))
    for copy in departures:
        copy.wait()


def own_kernel(mine_ref, gap_row_ref, gap_col_ref, high_ref, low_ref, gamma_ref, stage_ref, sem):
    rows, width = mine_ref.shape
    for at, cols in enumerate(panels(width)):
        fetch(mine_ref.at[:, cols], stage_ref.at[:, cols], sem.at[at])

    def gather(at, cols, state):
        integral, cross = state
        pltpu.make_async_copy(mine_ref.at[:, cols], stage_ref.at[:, cols], sem.at[at]).wait()
        high, low = halves(stage_ref[:, cols])
        high_ref[:, cols] = high
        low_ref[:, cols] = low
        return integral + mxu(high, high, NT), cross + mxu(high, low, NT)

    zero = jnp.zeros((rows, rows), jnp.float32)
    integral, cross = over_panels(width, gather, (zero, zero))
    integral = integral + (cross + cross.T)
    a_high, a_low = halves(integral / (gap_row_ref[...] + gap_col_ref[...]))

    def spread(at, cols, state):
        high, low = high_ref[:, cols], low_ref[:, cols]
        gamma_ref[:, cols] = mxu(a_high, high) + (mxu(a_high, low) + mxu(a_low, high))
        return state

    over_panels(width, spread, 0)


def step_kernel(plan, *refs):
    count, inner_rows, gaps, final, unroll = plan
    refs = list(refs)
    take = lambda number: [refs.pop(0) for _ in range(number)]
    others = take(count)
    high_ref, low_ref, gap_row_ref, table_ref = take(4)
    start_ref = take(1)[0]
    inner_ref = take(1)[0] if inner_rows else None
    gamma_ref, both_ref = take(2)
    if inner_rows:
        inner_stage_ref, inner_sem = take(2)
        at, height = inner_rows
        fetch(inner_ref.at[pl.ds(at, height)], inner_stage_ref, inner_sem).wait()
        others.append(inner_stage_ref)
    rows, width = high_ref.shape
    extent = both_ref.shape[0] // 2

    def gather(at, cols, state):
        main, rest = state
        high, low = halves(jnp.concatenate([ref[:, cols] for ref in others], axis=0))
        both = jnp.concatenate([high, low], axis=0)
        both_ref[:, cols] = both
        return main + mxu(high_ref[:, cols], both, NT), rest + mxu(low_ref[:, cols], high, NT)

    start = (jnp.zeros((rows, 2 * extent), jnp.float32), jnp.zeros((rows, extent), jnp.float32))
    main, rest = over_panels(width, gather, start, unroll)
    integral = main[:, :extent] + (main[:, extent:] + rest)
    gap_col = jnp.concatenate(
        [table_ref[row : row + 1, at : at + height] for row, at, height in gaps], axis=1
    )
    a_high, a_low = halves(integral / (gap_row_ref[...] + gap_col))
    a_twice = jnp.concatenate([a_high, a_high], axis=1)

    def spread(at, cols, state):
        both = both_ref[:, cols]
        gamma = start_ref[:, cols] + (mxu(a_twice, both) + mxu(a_low, both[:extent]))
        if final:
            stage_ref, sem = refs
            stage_ref[:, cols] = gamma
            fetch(stage_ref.at[:, cols], gamma_ref.at[:, cols], sem.at[at])
        else:
            gamma_ref[:, cols] = gamma
        return state

    over_panels(width, spread, 0, unroll)
    if final:
        stage_ref, sem = refs
        for at, cols in enumerate(panels(width)):
            pltpu.make_async_copy(stage_ref.at[:, cols], gamma_ref.at[:, cols], sem.at[at]).wait()


VMEM = pl.BlockSpec(memory_space=pltpu.VMEM)
HBM = pl.BlockSpec(memory_space=pltpu.HBM)


def cost(rows, extent, width):
    return pl.CostEstimate(flops=12 * rows * extent * width, bytes_accessed=4 * extent * width, transcendentals=0)


def in_vmem(array):
    return pltpu.with_memory_space_constraint(array, pltpu.VMEM)


def in_hbm(array):
    return pltpu.with_memory_space_constraint(array, pltpu.HBM)


def params(mebibytes):
    return pltpu.CompilerParams(vmem_limit_bytes=mebibytes << 20)


def cut_call(mine, ranges):
    width = mine.shape[1]
    count = len(ranges)
    return pl.pallas_call(
        functools.partial(cut_kernel, [start for start, _ in ranges]),
        out_shape=tuple(pltpu.VMEM((height, width), jnp.float32) for _, height in ranges),
        in_specs=[HBM],
        out_specs=(VMEM,) * count,
        scratch_shapes=[pltpu.SemaphoreType.DMA((count,))],
        compiler_params=params(2),
        cost_estimate=pl.CostEstimate(flops=0, bytes_accessed=1 << 20, transcendentals=0),
        name="first_cuts",
    )(in_hbm(mine))


def split_call(mine, ranges):
    rows, width = mine.shape
    count = len(ranges)
    return pl.pallas_call(
        functools.partial(split_kernel, [start for start, _ in ranges]),
        out_shape=tuple(pltpu.HBM((height, width), jnp.float32) for _, height in ranges),
        in_specs=[HBM],
        out_specs=(HBM,) * count,
        scratch_shapes=[
            pltpu.VMEM((rows, width), jnp.float32),
            pltpu.SemaphoreType.DMA((count,)),
            pltpu.SemaphoreType.DMA((count,)),
        ],
        compiler_params=params(6),
        cost_estimate=cost(rows, rows, width),
        name="other_cuts",
    )(in_hbm(mine))


def own_call(mine, gap_row, gap_col):
    rows, width = mine.shape
    factor = pltpu.VMEM((rows, width), jnp.bfloat16)
    return pl.pallas_call(
        own_kernel,
        out_shape=(factor, factor, pltpu.VMEM((rows, width), jnp.float32)),
        in_specs=[HBM, VMEM, VMEM],
        out_specs=(VMEM,) * 3,
        scratch_shapes=[
            pltpu.VMEM((rows, width), jnp.float32),
            pltpu.SemaphoreType.DMA((width // PANEL,)),
        ],
        compiler_params=params(10),
        cost_estimate=pl.CostEstimate(flops=1 << 20, bytes_accessed=1 << 16, transcendentals=0),
        name="own_block",
    )(in_hbm(mine), gap_row, gap_col)


def step_call(others, high, low, gap_row, table, gaps, begin, inner, inner_rows, final, unroll, name):
    rows, width = high.shape
    extent = sum(other.shape[0] for other in others)
    scratch = []
    if inner_rows:
        extent += inner_rows[1]
        scratch += [pltpu.VMEM((inner_rows[1], width), jnp.float32), pltpu.SemaphoreType.DMA]
    if final:
        scratch += [pltpu.VMEM((rows, width), jnp.float32), pltpu.SemaphoreType.DMA((width // PANEL,))]
    extra = [in_hbm(inner)] if inner_rows else []
    return pl.pallas_call(
        functools.partial(step_kernel, (len(others), inner_rows, gaps, final, unroll)),
        out_shape=(pltpu.HBM if final else pltpu.VMEM)((rows, width), jnp.float32),
        in_specs=[VMEM] * (len(others) + 5) + [HBM] * len(extra),
        out_specs=HBM if final else VMEM,
        scratch_shapes=[pltpu.VMEM((2 * extent, width), jnp.bfloat16)] + scratch,
        input_output_aliases={} if final else {len(others) + 4: 0},
        compiler_params=params(10),
        cost_estimate=pl.CostEstimate(flops=1 << 20, bytes_accessed=1 << 16, transcendentals=0),
        name=name,
    )(*map(in_vmem, others), in_vmem(high), in_vmem(low), gap_row, table, in_vmem(begin), *extra)


def local(b_factors, occ_energy, vir_energy):
    occ_block, vir_block, width = b_factors.shape
    occ_count = lax.axis_size("occ")
    vir_count = lax.axis_size("vir")
    occ_here = lax.axis_index("occ")
    vir_here = lax.axis_index("vir")

    def moved(block, target):
        route = []
        for occ in range(occ_count):
            for vir in range(vir_count):
                occ_to, vir_to = target(occ, vir)
                route.append(
                    (occ * vir_count + vir, occ_to % occ_count * vir_count + vir_to % vir_count)
                )
        return lax.ppermute(block, AXES, route)

    def across(occ, vir):
        return occ ^ 1, vir

    def back(occ, vir):
        return (occ + 2 if occ % 2 else occ - 2), vir

    def along(occ, vir):
        return (occ - 2 if occ % 2 else occ + 2), vir

    def outward(occ, vir):
        return occ ^ 1, (vir + 1 if vir % 2 else vir - 1)

    def inward(occ, vir):
        return occ, vir ^ 1

    def gap_of(occ_place, vir_place):
        occ_part = lax.dynamic_slice_in_dim(
            occ_energy, occ_place % occ_count * occ_block, occ_block
        )
        vir_part = lax.dynamic_slice_in_dim(
            vir_energy, vir_place % vir_count * vir_block, vir_block
        )
        return occ_part[:, None] - vir_part[None, :]

    occ_side = 1 - 2 * (occ_here % 2)
    vir_side = 1 - 2 * (vir_here % 2)
    gap = gap_of(occ_here, vir_here)
    gap_inner = gap_of(occ_here, vir_here + vir_side)
    gap_near = gap_of(occ_here + occ_side, vir_here)
    gap_far = gap_of(occ_here + occ_count - occ_side, vir_here)
    gap_outer = gap_of(occ_here, vir_here + vir_count - vir_side)
    gap_row = gap.reshape(-1, 1)
    table = jnp.concatenate([gap_near, gap_far, gap_outer, gap_inner], axis=1)

    def held(value, *earlier):
        return lax.optimization_barrier((value, earlier))[0]

    mine = b_factors.reshape(occ_block * vir_block, width)
    size = mine.shape[0]
    early = vir_block // 2
    count = occ_block
    ranges = [(k * vir_block, vir_block) for k in range(count)]

    first, ahead = cut_call(mine, [ranges[0], (size - early, early)])
    parts = [first]
    near = [moved(first, across)]
    inner = moved(b_factors, inward).reshape(size, width)
    ahead_back, ahead_out = moved(ahead, back), moved(ahead, outward)
    parts += split_call(held(mine, first), ranges[1:])
    near.append(moved(held(parts[1], ahead_back, ahead_out), across))
    high, low, gamma = own_call(held(mine, near[0], inner), gap_row, gap.reshape(1, -1))

    done = [parts[1], gamma]
    far, outer = [], []
    begin = gamma
    inner_at = 0

    def step(k, *earlier):
        nonlocal begin, inner_at
        final = k == count - 1
        others = [near[k], far[k], outer[k]]
        rows = None
        if final:
            others.append(late)
            at = vir_block - early
            gaps = [(k, 0, vir_block)]
            gaps += [(k, which * vir_block + shift, early) for shift in (0, at) for which in (1, 2)]
        else:
            others = [held(other, *earlier) for other in others]
            height = INNER_ROWS[k] * vir_block
            rows = (inner_at, height) if height else None
            gaps = [(k, 0, 3 * vir_block)]
            gaps += [(row, 3 * vir_block, vir_block) for row in range(inner_at // vir_block, (inner_at + height) // vir_block)]
            inner_at += height
        gamma = step_call(others, high, low, gap_row, table, gaps, begin, inner, rows, final, 4 if k > 3 else 2, "step_%d" % k)
        begin = gamma
        done.append(gamma)
        return gamma

    late = None
    for k in range(count):
        part = held(near[k], done[k])
        if k == count - 1:
            part = part[: vir_block - early]
        far.append(moved(part, along))
        outer.append(moved(part, outward))
        if k + 2 < count:
            near.append(moved(held(parts[k + 2], part), across))
        elif k + 2 == count:
            relayed = held(jnp.concatenate([ahead_back, ahead_out], axis=0), part, far[k - 1], outer[k - 1])
            late = moved(relayed, across)
        if k > 0:
            step(k - 1, part)
    gamma = step(count - 1)
    return gamma.reshape(occ_block, vir_block, width)


def solution(mesh):
    in_specs = (P("occ", "vir", None), P(), P())
    out_specs = P("occ", "vir", None)
    return jax.shard_map(local, mesh=mesh, in_specs=in_specs, out_specs=out_specs, check_vma=False)
```

```python
import functools
import jax
import jax.numpy as jnp
from jax import lax
from jax.experimental import pallas as pl
from jax.experimental.pallas import tpu as pltpu
from jax.sharding import PartitionSpec as P

AXES = ("occ", "vir")
PANEL = 1024
INNER_ROWS = (1, 1, 1, 1, 2, 2, 0)
NT = (((1,), (1,)), ((), ()))
NN = (((1,), (0,)), ((), ()))


def mxu(left, right, dims=NN):
    return lax.dot_general(left, right, dims, preferred_element_type=jnp.float32)


def halves(value):
    high = value.astype(jnp.bfloat16)
    low = (value - high.astype(jnp.float32)).astype(jnp.bfloat16)
    return high, low


def panels(width):
    return [slice(at, at + PANEL) for at in range(0, width, PANEL)]


def fetch(source_ref, target_ref, sem):
    copy = pltpu.make_async_copy(source_ref, target_ref, sem)
    copy.start()
    return copy


def row_cuts(mine_ref, targets, starts, sem):
    copies = []
    for at, (target, start) in enumerate(zip(targets, starts)):
        rows = pl.ds(start, target.shape[0])
        copies.append(fetch(mine_ref.at[rows], target, sem.at[at]))
    return copies


def cut_kernel(starts, mine_ref, *refs):
    for copy in row_cuts(mine_ref, refs[:-1], starts, refs[-1]):
        copy.wait()


def over_panels(width, body, start, unroll=2):
    def turn(at, state):
        return body(at, pl.ds(pl.multiple_of(at * PANEL, PANEL), PANEL), state)

    return lax.fori_loop(0, width // PANEL, turn, start, unroll=unroll)


def split_kernel(starts, mine_ref, *refs):
    *parts, stage_ref, in_sem, out_sem = refs
    arrivals, departures = [], []
    for at, (part, start) in enumerate(zip(parts, starts)):
        rows = pl.ds(start, part.shape[0])
        arrivals.append(fetch(mine_ref.at[rows], stage_ref.at[rows], in_sem.at[at]))
    for at, (part, start) in enumerate(zip(parts, starts)):
        arrivals[at].wait()
        departures.append(fetch(stage_ref.at[pl.ds(start, part.shape[0])], part, out_sem.at[at]))
    for copy in departures:
        copy.wait()


def own_kernel(mine_ref, gap_row_ref, gap_col_ref, high_ref, low_ref, gamma_ref, stage_ref, sem):
    rows, width = mine_ref.shape
    for at, cols in enumerate(panels(width)):
        fetch(mine_ref.at[:, cols], stage_ref.at[:, cols], sem.at[at])

    def gather(at, cols, state):
        integral, cross = state
        pltpu.make_async_copy(mine_ref.at[:, cols], stage_ref.at[:, cols], sem.at[at]).wait()
        high, low = halves(stage_ref[:, cols])
        high_ref[:, cols] = high
        low_ref[:, cols] = low
        return integral + mxu(high, high, NT), cross + mxu(high, low, NT)

    zero = jnp.zeros((rows, rows), jnp.float32)
    integral, cross = over_panels(width, gather, (zero, zero))
    integral = integral + (cross + cross.T)
    a_high, a_low = halves(integral / (gap_row_ref[...] + gap_col_ref[...]))

    def spread(at, cols, state):
        high, low = high_ref[:, cols], low_ref[:, cols]
        gamma_ref[:, cols] = mxu(a_high, high) + (mxu(a_high, low) + mxu(a_low, high))
        return state

    over_panels(width, spread, 0)


def step_kernel(plan, *refs):
    count, inner_rows, gaps, final, unroll = plan
    refs = list(refs)
    take = lambda number: [refs.pop(0) for _ in range(number)]
    others = take(count)
    high_ref, low_ref, gap_row_ref, table_ref = take(4)
    start_ref = take(1)[0]
    inner_ref = take(1)[0] if inner_rows else None
    gamma_ref, both_ref = take(2)
    if inner_rows:
        inner_stage_ref, inner_sem = take(2)
        at, height = inner_rows
        fetch(inner_ref.at[pl.ds(at, height)], inner_stage_ref, inner_sem).wait()
        others.append(inner_stage_ref)
    rows, width = high_ref.shape
    extent = both_ref.shape[0] // 2

    def gather(at, cols, state):
        main, rest = state
        high, low = halves(jnp.concatenate([ref[:, cols] for ref in others], axis=0))
        both = jnp.concatenate([high, low], axis=0)
        both_ref[:, cols] = both
        return main + mxu(high_ref[:, cols], both, NT), rest + mxu(low_ref[:, cols], high, NT)

    start = (jnp.zeros((rows, 2 * extent), jnp.float32), jnp.zeros((rows, extent), jnp.float32))
    main, rest = over_panels(width, gather, start, unroll)
    integral = main[:, :extent] + (main[:, extent:] + rest)
    gap_col = jnp.concatenate(
        [table_ref[row : row + 1, at : at + height] for row, at, height in gaps], axis=1
    )
    a_high, a_low = halves(integral / (gap_row_ref[...] + gap_col))
    a_twice = jnp.concatenate([a_high, a_high], axis=1)

    def spread(at, cols, state):
        both = both_ref[:, cols]
        gamma = start_ref[:, cols] + (mxu(a_twice, both) + mxu(a_low, both[:extent]))
        if final:
            stage_ref, sem = refs
            stage_ref[:, cols] = gamma
            fetch(stage_ref.at[:, cols], gamma_ref.at[:, cols], sem.at[at])
        else:
            gamma_ref[:, cols] = gamma
        return state

    over_panels(width, spread, 0, unroll)
    if final:
        stage_ref, sem = refs
        for at, cols in enumerate(panels(width)):
            pltpu.make_async_copy(stage_ref.at[:, cols], gamma_ref.at[:, cols], sem.at[at]).wait()


VMEM = pl.BlockSpec(memory_space=pltpu.VMEM)
HBM = pl.BlockSpec(memory_space=pltpu.HBM)


def cost(rows, extent, width):
    return pl.CostEstimate(flops=12 * rows * extent * width, bytes_accessed=4 * extent * width, transcendentals=0)


def in_vmem(array):
    return pltpu.with_memory_space_constraint(array, pltpu.VMEM)


def in_hbm(array):
    return pltpu.with_memory_space_constraint(array, pltpu.HBM)


def params(mebibytes):
    return pltpu.CompilerParams(vmem_limit_bytes=mebibytes << 20)


def cut_call(mine, ranges):
    width = mine.shape[1]
    count = len(ranges)
    return pl.pallas_call(
        functools.partial(cut_kernel, [start for start, _ in ranges]),
        out_shape=tuple(pltpu.VMEM((height, width), jnp.float32) for _, height in ranges),
        in_specs=[HBM],
        out_specs=(VMEM,) * count,
        scratch_shapes=[pltpu.SemaphoreType.DMA((count,))],
        compiler_params=params(2),
        cost_estimate=pl.CostEstimate(flops=0, bytes_accessed=1 << 20, transcendentals=0),
        name="first_cuts",
    )(in_hbm(mine))


def split_call(mine, ranges):
    rows, width = mine.shape
    count = len(ranges)
    return pl.pallas_call(
        functools.partial(split_kernel, [start for start, _ in ranges]),
        out_shape=tuple(pltpu.HBM((height, width), jnp.float32) for _, height in ranges),
        in_specs=[HBM],
        out_specs=(HBM,) * count,
        scratch_shapes=[
            pltpu.VMEM((rows, width), jnp.float32),
            pltpu.SemaphoreType.DMA((count,)),
            pltpu.SemaphoreType.DMA((count,)),
        ],
        compiler_params=params(6),
        cost_estimate=cost(rows, rows, width),
        name="other_cuts",
    )(in_hbm(mine))


def own_call(mine, gap_row, gap_col):
    rows, width = mine.shape
    factor = pltpu.VMEM((rows, width), jnp.bfloat16)
    return pl.pallas_call(
        own_kernel,
        out_shape=(factor, factor, pltpu.VMEM((rows, width), jnp.float32)),
        in_specs=[HBM, VMEM, VMEM],
        out_specs=(VMEM,) * 3,
        scratch_shapes=[
            pltpu.VMEM((rows, width), jnp.float32),
            pltpu.SemaphoreType.DMA((width // PANEL,)),
        ],
        compiler_params=params(10),
        cost_estimate=pl.CostEstimate(flops=1 << 20, bytes_accessed=1 << 16, transcendentals=0),
        name="own_block",
    )(in_hbm(mine), gap_row, gap_col)


def step_call(others, high, low, gap_row, table, gaps, begin, inner, inner_rows, final, unroll, name):
    rows, width = high.shape
    extent = sum(other.shape[0] for other in others)
    scratch = []
    if inner_rows:
        extent += inner_rows[1]
        scratch += [pltpu.VMEM((inner_rows[1], width), jnp.float32), pltpu.SemaphoreType.DMA]
    if final:
        scratch += [pltpu.VMEM((rows, width), jnp.float32), pltpu.SemaphoreType.DMA((width // PANEL,))]
    extra = [in_hbm(inner)] if inner_rows else []
    return pl.pallas_call(
        functools.partial(step_kernel, (len(others), inner_rows, gaps, final, unroll)),
        out_shape=(pltpu.HBM if final else pltpu.VMEM)((rows, width), jnp.float32),
        in_specs=[VMEM] * (len(others) + 5) + [HBM] * len(extra),
        out_specs=HBM if final else VMEM,
        scratch_shapes=[pltpu.VMEM((2 * extent, width), jnp.bfloat16)] + scratch,
        input_output_aliases={} if final else {len(others) + 4: 0},
        compiler_params=params(10),
        cost_estimate=pl.CostEstimate(flops=1 << 20, bytes_accessed=1 << 16, transcendentals=0),
        name=name,
    )(*map(in_vmem, others), in_vmem(high), in_vmem(low), gap_row, table, in_vmem(begin), *extra)


def local(b_factors, occ_energy, vir_energy):
    occ_block, vir_block, width = b_factors.shape
    occ_count = lax.axis_size("occ")
    vir_count = lax.axis_size("vir")
    occ_here = lax.axis_index("occ")
    vir_here = lax.axis_index("vir")

    def moved(block, target):
        route = []
        for occ in range(occ_count):
            for vir in range(vir_count):
                occ_to, vir_to = target(occ, vir)
                route.append(
                    (occ * vir_count + vir, occ_to % occ_count * vir_count + vir_to % vir_count)
                )
        return lax.ppermute(block, AXES, route)

    def across(occ, vir):
        return occ ^ 1, vir

    def back(occ, vir):
        return (occ + 2 if occ % 2 else occ - 2), vir

    def along(occ, vir):
        return (occ - 2 if occ % 2 else occ + 2), vir

    def outward(occ, vir):
        return occ ^ 1, (vir + 1 if vir % 2 else vir - 1)

    def inward(occ, vir):
        return occ, vir ^ 1

    def gap_of(occ_place, vir_place):
        occ_part = lax.dynamic_slice_in_dim(
            occ_energy, occ_place % occ_count * occ_block, occ_block
        )
        vir_part = lax.dynamic_slice_in_dim(
            vir_energy, vir_place % vir_count * vir_block, vir_block
        )
        return occ_part[:, None] - vir_part[None, :]

    occ_side = 1 - 2 * (occ_here % 2)
    vir_side = 1 - 2 * (vir_here % 2)
    gap = gap_of(occ_here, vir_here)
    gap_inner = gap_of(occ_here, vir_here + vir_side)
    gap_near = gap_of(occ_here + occ_side, vir_here)
    gap_far = gap_of(occ_here + occ_count - occ_side, vir_here)
    gap_outer = gap_of(occ_here, vir_here + vir_count - vir_side)
    gap_row = gap.reshape(-1, 1)
    table = jnp.concatenate([gap_near, gap_far, gap_outer, gap_inner], axis=1)

    def held(value, *earlier):
        return lax.optimization_barrier((value, earlier))[0]

    mine = b_factors.reshape(occ_block * vir_block, width)
    size = mine.shape[0]
    early = vir_block // 2
    count = occ_block
    ranges = [(k * vir_block, vir_block) for k in range(count)]

    first, ahead = cut_call(mine, [ranges[0], (size - early, early)])
    parts = [first]
    near = [moved(first, across)]
    inner = moved(b_factors, inward).reshape(size, width)
    ahead_back, ahead_out = moved(ahead, back), moved(ahead, outward)
    parts += split_call(held(mine, first), ranges[1:])
    near.append(moved(parts[1], across))
    high, low, gamma = own_call(held(mine, near[0], inner), gap_row, gap.reshape(1, -1))

    done = [parts[1], gamma]
    far, outer = [], []
    begin = gamma
    inner_at = 0

    def step(k, *earlier):
        nonlocal begin, inner_at
        final = k == count - 1
        others = [near[k], far[k], outer[k]]
        rows = None
        if final:
            others.append(late)
            at = vir_block - early
            gaps = [(k, 0, vir_block)]
            gaps += [(k, which * vir_block + shift, early) for shift in (0, at) for which in (1, 2)]
        else:
            others = [held(other, *earlier) for other in others]
            height = INNER_ROWS[k] * vir_block
            rows = (inner_at, height) if height else None
            gaps = [(k, 0, 3 * vir_block)]
            gaps += [(row, 3 * vir_block, vir_block) for row in range(inner_at // vir_block, (inner_at + height) // vir_block)]
            inner_at += height
        gamma = step_call(others, high, low, gap_row, table, gaps, begin, inner, rows, final, 4 if k > 3 else 2, "step_%d" % k)
        begin = gamma
        done.append(gamma)
        return gamma

    relayed = jnp.concatenate([ahead_back, ahead_out], axis=0)
    for k in range(count):
        part = held(near[k], done[k])
        if k == 0:
            part = held(part, ahead_back, ahead_out)
        if k == 1:
            part = held(part, relayed)
        if k == count - 1:
            part = part[: vir_block - early]
        far.append(moved(part, along))
        outer.append(moved(part, outward))
        if k + 2 < count:
            near.append(moved(held(parts[k + 2], part), across))
        elif k + 2 == count:
            late = moved(held(relayed, part, far[k - 1], outer[k - 1]), across)
        if k > 0:
            step(k - 1, part)
    gamma = step(count - 1)
    return gamma.reshape(occ_block, vir_block, width)


def solution(mesh):
    in_specs = (P("occ", "vir", None), P(), P())
    out_specs = P("occ", "vir", None)
    return jax.shard_map(local, mesh=mesh, in_specs=in_specs, out_specs=out_specs, check_vma=False)
```

```python
import functools
import jax
import jax.numpy as jnp
from jax import lax
from jax.experimental import pallas as pl
from jax.experimental.pallas import tpu as pltpu
from jax.sharding import PartitionSpec as P

AXES = ("occ", "vir")
PANEL = 1024
INNER_ROWS = (1, 1, 1, 1, 2, 2, 0)
NT = (((1,), (1,)), ((), ()))
NN = (((1,), (0,)), ((), ()))


def mxu(left, right, dims=NN):
    return lax.dot_general(left, right, dims, preferred_element_type=jnp.float32)


def halves(value):
    high = value.astype(jnp.bfloat16)
    low = (value - high.astype(jnp.float32)).astype(jnp.bfloat16)
    return high, low


def panels(width):
    return [slice(at, at + PANEL) for at in range(0, width, PANEL)]


def fetch(source_ref, target_ref, sem):
    copy = pltpu.make_async_copy(source_ref, target_ref, sem)
    copy.start()
    return copy


def row_cuts(mine_ref, targets, starts, sem):
    copies = []
    for at, (target, start) in enumerate(zip(targets, starts)):
        rows = pl.ds(start, target.shape[0])
        copies.append(fetch(mine_ref.at[rows], target, sem.at[at]))
    return copies


def cut_kernel(starts, mine_ref, *refs):
    for copy in row_cuts(mine_ref, refs[:-1], starts, refs[-1]):
        copy.wait()


def over_panels(width, body, start, unroll=2):
    def turn(at, state):
        return body(at, pl.ds(pl.multiple_of(at * PANEL, PANEL), PANEL), state)

    return lax.fori_loop(0, width // PANEL, turn, start, unroll=unroll)


def split_kernel(starts, mine_ref, *refs):
    *parts, stage_ref, in_sem, out_sem = refs
    arrivals, departures = [], []
    reached = starts[0]
    for at, (part, start) in enumerate(zip(parts, starts)):
        if start >= reached:
            reached = start + part.shape[0]
            rows = pl.ds(start, part.shape[0])
            arrivals.append(fetch(mine_ref.at[rows], stage_ref.at[rows], in_sem.at[at]))
    for at, (part, start) in enumerate(zip(parts, starts)):
        if at < len(arrivals):
            arrivals[at].wait()
        departures.append(fetch(stage_ref.at[pl.ds(start, part.shape[0])], part, out_sem.at[at]))
    for copy in departures:
        copy.wait()


def own_kernel(mine_ref, gap_row_ref, gap_col_ref, high_ref, low_ref, gamma_ref, stage_ref, sem):
    rows, width = mine_ref.shape
    for at, cols in enumerate(panels(width)):
        fetch(mine_ref.at[:, cols], stage_ref.at[:, cols], sem.at[at])

    def gather(at, cols, state):
        integral, cross = state
        pltpu.make_async_copy(mine_ref.at[:, cols], stage_ref.at[:, cols], sem.at[at]).wait()
        high, low = halves(stage_ref[:, cols])
        high_ref[:, cols] = high
        low_ref[:, cols] = low
        return integral + mxu(high, high, NT), cross + mxu(high, low, NT)

    zero = jnp.zeros((rows, rows), jnp.float32)
    integral, cross = over_panels(width, gather, (zero, zero))
    integral = integral + (cross + cross.T)
    a_high, a_low = halves(integral / (gap_row_ref[...] + gap_col_ref[...]))

    def spread(at, cols, state):
        high, low = high_ref[:, cols], low_ref[:, cols]
        gamma_ref[:, cols] = mxu(a_high, high) + (mxu(a_high, low) + mxu(a_low, high))
        return state

    over_panels(width, spread, 0)


def step_kernel(plan, *refs):
    count, inner_rows, gaps, final, unroll = plan
    refs = list(refs)
    take = lambda number: [refs.pop(0) for _ in range(number)]
    others = take(count)
    high_ref, low_ref, gap_row_ref, table_ref = take(4)
    start_ref = take(1)[0]
    inner_ref = take(1)[0] if inner_rows else None
    gamma_ref, both_ref = take(2)
    if inner_rows:
        inner_stage_ref, inner_sem = take(2)
        at, height = inner_rows
        fetch(inner_ref.at[pl.ds(at, height)], inner_stage_ref, inner_sem).wait()
        others.append(inner_stage_ref)
    rows, width = high_ref.shape
    extent = both_ref.shape[0] // 2

    def gather(at, cols, state):
        main, rest = state
        high, low = halves(jnp.concatenate([ref[:, cols] for ref in others], axis=0))
        both = jnp.concatenate([high, low], axis=0)
        both_ref[:, cols] = both
        return main + mxu(high_ref[:, cols], both, NT), rest + mxu(low_ref[:, cols], high, NT)

    start = (jnp.zeros((rows, 2 * extent), jnp.float32), jnp.zeros((rows, extent), jnp.float32))
    main, rest = over_panels(width, gather, start, unroll)
    integral = main[:, :extent] + (main[:, extent:] + rest)
    gap_col = jnp.concatenate(
        [table_ref[row : row + 1, at : at + height] for row, at, height in gaps], axis=1
    )
    a_high, a_low = halves(integral / (gap_row_ref[...] + gap_col))
    a_twice = jnp.concatenate([a_high, a_high], axis=1)

    def spread(at, cols, state):
        both = both_ref[:, cols]
        gamma = start_ref[:, cols] + (mxu(a_twice, both) + mxu(a_low, both[:extent]))
        if final:
            stage_ref, sem = refs
            stage_ref[:, cols] = gamma
            fetch(stage_ref.at[:, cols], gamma_ref.at[:, cols], sem.at[at])
        else:
            gamma_ref[:, cols] = gamma
        return state

    over_panels(width, spread, 0, unroll)
    if final:
        stage_ref, sem = refs
        for at, cols in enumerate(panels(width)):
            pltpu.make_async_copy(stage_ref.at[:, cols], gamma_ref.at[:, cols], sem.at[at]).wait()


VMEM = pl.BlockSpec(memory_space=pltpu.VMEM)
HBM = pl.BlockSpec(memory_space=pltpu.HBM)


def cost(rows, extent, width):
    return pl.CostEstimate(flops=12 * rows * extent * width, bytes_accessed=4 * extent * width, transcendentals=0)


def in_vmem(array):
    return pltpu.with_memory_space_constraint(array, pltpu.VMEM)


def in_hbm(array):
    return pltpu.with_memory_space_constraint(array, pltpu.HBM)


def params(mebibytes):
    return pltpu.CompilerParams(vmem_limit_bytes=mebibytes << 20)


def cut_call(mine, ranges):
    width = mine.shape[1]
    count = len(ranges)
    return pl.pallas_call(
        functools.partial(cut_kernel, [start for start, _ in ranges]),
        out_shape=tuple(pltpu.VMEM((height, width), jnp.float32) for _, height in ranges),
        in_specs=[HBM],
        out_specs=(VMEM,) * count,
        scratch_shapes=[pltpu.SemaphoreType.DMA((count,))],
        compiler_params=params(2),
        cost_estimate=pl.CostEstimate(flops=0, bytes_accessed=1 << 20, transcendentals=0),
        name="first_cuts",
    )(in_hbm(mine))


def split_call(mine, ranges):
    rows, width = mine.shape
    count = len(ranges)
    return pl.pallas_call(
        functools.partial(split_kernel, [start for start, _ in ranges]),
        out_shape=tuple(pltpu.HBM((height, width), jnp.float32) for _, height in ranges),
        in_specs=[HBM],
        out_specs=(HBM,) * count,
        scratch_shapes=[
            pltpu.VMEM((rows, width), jnp.float32),
            pltpu.SemaphoreType.DMA((count,)),
            pltpu.SemaphoreType.DMA((count,)),
        ],
        compiler_params=params(6),
        cost_estimate=cost(rows, rows, width),
        name="other_cuts",
    )(in_hbm(mine))


def own_call(mine, gap_row, gap_col):
    rows, width = mine.shape
    factor = pltpu.VMEM((rows, width), jnp.bfloat16)
    return pl.pallas_call(
        own_kernel,
        out_shape=(factor, factor, pltpu.VMEM((rows, width), jnp.float32)),
        in_specs=[HBM, VMEM, VMEM],
        out_specs=(VMEM,) * 3,
        scratch_shapes=[
            pltpu.VMEM((rows, width), jnp.float32),
            pltpu.SemaphoreType.DMA((width // PANEL,)),
        ],
        compiler_params=params(10),
        cost_estimate=pl.CostEstimate(flops=1 << 20, bytes_accessed=1 << 16, transcendentals=0),
        name="own_block",
    )(in_hbm(mine), gap_row, gap_col)


def step_call(others, high, low, gap_row, table, gaps, begin, inner, inner_rows, final, unroll, name):
    rows, width = high.shape
    extent = sum(other.shape[0] for other in others)
    scratch = []
    if inner_rows:
        extent += inner_rows[1]
        scratch += [pltpu.VMEM((inner_rows[1], width), jnp.float32), pltpu.SemaphoreType.DMA]
    if final:
        scratch += [pltpu.VMEM((rows, width), jnp.float32), pltpu.SemaphoreType.DMA((width // PANEL,))]
    extra = [in_hbm(inner)] if inner_rows else []
    return pl.pallas_call(
        functools.partial(step_kernel, (len(others), inner_rows, gaps, final, unroll)),
        out_shape=(pltpu.HBM if final else pltpu.VMEM)((rows, width), jnp.float32),
        in_specs=[VMEM] * (len(others) + 5) + [HBM] * len(extra),
        out_specs=HBM if final else VMEM,
        scratch_shapes=[pltpu.VMEM((2 * extent, width), jnp.bfloat16)] + scratch,
        input_output_aliases={} if final else {len(others) + 4: 0},
        compiler_params=params(10),
        cost_estimate=pl.CostEstimate(flops=1 << 20, bytes_accessed=1 << 16, transcendentals=0),
        name=name,
    )(*map(in_vmem, others), in_vmem(high), in_vmem(low), gap_row, table, in_vmem(begin), *extra)


def local(b_factors, occ_energy, vir_energy):
    occ_block, vir_block, width = b_factors.shape
    occ_count = lax.axis_size("occ")
    vir_count = lax.axis_size("vir")
    occ_here = lax.axis_index("occ")
    vir_here = lax.axis_index("vir")

    def moved(block, target):
        route = []
        for occ in range(occ_count):
            for vir in range(vir_count):
                occ_to, vir_to = target(occ, vir)
                route.append(
                    (occ * vir_count + vir, occ_to % occ_count * vir_count + vir_to % vir_count)
                )
        return lax.ppermute(block, AXES, route)

    def across(occ, vir):
        return occ ^ 1, vir

    def back(occ, vir):
        return (occ + 2 if occ % 2 else occ - 2), vir

    def along(occ, vir):
        return (occ - 2 if occ % 2 else occ + 2), vir

    def outward(occ, vir):
        return occ ^ 1, (vir + 1 if vir % 2 else vir - 1)

    def inward(occ, vir):
        return occ, vir ^ 1

    def gap_of(occ_place, vir_place):
        occ_part = lax.dynamic_slice_in_dim(
            occ_energy, occ_place % occ_count * occ_block, occ_block
        )
        vir_part = lax.dynamic_slice_in_dim(
            vir_energy, vir_place % vir_count * vir_block, vir_block
        )
        return occ_part[:, None] - vir_part[None, :]

    occ_side = 1 - 2 * (occ_here % 2)
    vir_side = 1 - 2 * (vir_here % 2)
    gap = gap_of(occ_here, vir_here)
    gap_inner = gap_of(occ_here, vir_here + vir_side)
    gap_near = gap_of(occ_here + occ_side, vir_here)
    gap_far = gap_of(occ_here + occ_count - occ_side, vir_here)
    gap_outer = gap_of(occ_here, vir_here + vir_count - vir_side)
    gap_row = gap.reshape(-1, 1)
    table = jnp.concatenate([gap_near, gap_far, gap_outer, gap_inner], axis=1)

    def held(value, *earlier):
        return lax.optimization_barrier((value, earlier))[0]

    mine = b_factors.reshape(occ_block * vir_block, width)
    size = mine.shape[0]
    early = vir_block // 2
    count = occ_block
    ranges = [(k * vir_block, vir_block) for k in range(count)]

    [first] = cut_call(mine, ranges[:1])
    parts = [first]
    near = [moved(first, across)]
    inner = moved(b_factors, inward).reshape(size, width)
    *rest, ahead = split_call(held(mine, first), ranges[1:] + [(size - early, early)])
    parts += rest
    near.append(moved(parts[1], across))
    ahead_back, ahead_out = moved(ahead, back), moved(ahead, outward)
    high, low, gamma = own_call(held(mine, near[0], inner), gap_row, gap.reshape(1, -1))

    done = [parts[1], gamma]
    far, outer = [], []
    begin = gamma
    inner_at = 0

    def step(k, *earlier):
        nonlocal begin, inner_at
        final = k == count - 1
        others = [near[k], far[k], outer[k]]
        rows = None
        if final:
            others.append(late)
            at = vir_block - early
            gaps = [(k, 0, vir_block)]
            gaps += [(k, which * vir_block + shift, early) for shift in (0, at) for which in (1, 2)]
        else:
            others = [held(other, *earlier) for other in others]
            height = INNER_ROWS[k] * vir_block
            rows = (inner_at, height) if height else None
            gaps = [(k, 0, 3 * vir_block)]
            gaps += [(row, 3 * vir_block, vir_block) for row in range(inner_at // vir_block, (inner_at + height) // vir_block)]
            inner_at += height
        gamma = step_call(others, high, low, gap_row, table, gaps, begin, inner, rows, final, 4 if k > 3 else 2, "step_%d" % k)
        begin = gamma
        done.append(gamma)
        return gamma

    relayed = jnp.concatenate([ahead_back, ahead_out], axis=0)
    for k in range(count):
        part = held(near[k], done[k])
        if k == 0:
            part = held(part, ahead_back, ahead_out)
        if k == 1:
            part = held(part, relayed)
        if k == count - 1:
            part = part[: vir_block - early]
        far.append(moved(part, along))
        outer.append(moved(part, outward))
        if k + 2 < count:
            near.append(moved(held(parts[k + 2], part), across))
        elif k + 2 == count:
            late = moved(held(relayed, part, far[k - 1], outer[k - 1]), across)
        if k > 0:
            step(k - 1, part)
    gamma = step(count - 1)
    return gamma.reshape(occ_block, vir_block, width)


def solution(mesh):
    in_specs = (P("occ", "vir", None), P(), P())
    out_specs = P("occ", "vir", None)
    return jax.shard_map(local, mesh=mesh, in_specs=in_specs, out_specs=out_specs, check_vma=False)
```

```python
import functools
import jax
import jax.numpy as jnp
from jax import lax
from jax.experimental import pallas as pl
from jax.experimental.pallas import tpu as pltpu
from jax.sharding import PartitionSpec as P

AXES = ("occ", "vir")
PANEL = 1024
INNER_ROWS = (1, 1, 1, 1, 2, 2, 0)
NT = (((1,), (1,)), ((), ()))
NN = (((1,), (0,)), ((), ()))


def mxu(left, right, dims=NN):
    return lax.dot_general(left, right, dims, preferred_element_type=jnp.float32)


def halves(value):
    high = value.astype(jnp.bfloat16)
    low = (value - high.astype(jnp.float32)).astype(jnp.bfloat16)
    return high, low


def panels(width):
    return [slice(at, at + PANEL) for at in range(0, width, PANEL)]


def fetch(source_ref, target_ref, sem):
    copy = pltpu.make_async_copy(source_ref, target_ref, sem)
    copy.start()
    return copy


def row_cuts(mine_ref, targets, starts, sem):
    copies = []
    for at, (target, start) in enumerate(zip(targets, starts)):
        rows = pl.ds(start, target.shape[0])
        copies.append(fetch(mine_ref.at[rows], target, sem.at[at]))
    return copies


def cut_kernel(starts, mine_ref, *refs):
    for copy in row_cuts(mine_ref, refs[:-1], starts, refs[-1]):
        copy.wait()


def over_panels(width, body, start, unroll=2):
    def turn(at, state):
        return body(at, pl.ds(pl.multiple_of(at * PANEL, PANEL), PANEL), state)

    return lax.fori_loop(0, width // PANEL, turn, start, unroll=unroll)


def split_kernel(starts, mine_ref, *refs):
    *parts, stage_ref, in_sem, out_sem = refs
    arrivals, departures = [], []
    reached = starts[0]
    for at, (part, start) in enumerate(zip(parts, starts)):
        if start >= reached:
            reached = start + part.shape[0]
            rows = pl.ds(start, part.shape[0])
            arrivals.append(fetch(mine_ref.at[rows], stage_ref.at[rows], in_sem.at[at]))
    for at, (part, start) in enumerate(zip(parts, starts)):
        if at < len(arrivals):
            arrivals[at].wait()
        departures.append(fetch(stage_ref.at[pl.ds(start, part.shape[0])], part, out_sem.at[at]))
    for copy in departures:
        copy.wait()


def own_kernel(mine_ref, gap_row_ref, gap_col_ref, high_ref, low_ref, gamma_ref, stage_ref, sem):
    rows, width = mine_ref.shape
    for at, cols in enumerate(panels(width)):
        fetch(mine_ref.at[:, cols], stage_ref.at[:, cols], sem.at[at])

    def gather(at, cols, state):
        integral, cross = state
        pltpu.make_async_copy(mine_ref.at[:, cols], stage_ref.at[:, cols], sem.at[at]).wait()
        high, low = halves(stage_ref[:, cols])
        high_ref[:, cols] = high
        low_ref[:, cols] = low
        return integral + mxu(high, high, NT), cross + mxu(high, low, NT)

    zero = jnp.zeros((rows, rows), jnp.float32)
    integral, cross = over_panels(width, gather, (zero, zero))
    integral = integral + (cross + cross.T)
    a_high, a_low = halves(integral / (gap_row_ref[...] + gap_col_ref[...]))

    def spread(at, cols, state):
        high, low = high_ref[:, cols], low_ref[:, cols]
        gamma_ref[:, cols] = mxu(a_high, high) + (mxu(a_high, low) + mxu(a_low, high))
        return state

    over_panels(width, spread, 0)


def step_kernel(plan, *refs):
    count, inner_rows, gaps, final, unroll = plan
    refs = list(refs)
    take = lambda number: [refs.pop(0) for _ in range(number)]
    others = take(count)
    high_ref, low_ref, gap_row_ref, table_ref = take(4)
    start_ref = take(1)[0]
    inner_ref = take(1)[0] if inner_rows else None
    gamma_ref, both_ref = take(2)
    if inner_rows:
        inner_stage_ref, inner_sem = take(2)
        at, height = inner_rows
        fetch(inner_ref.at[pl.ds(at, height)], inner_stage_ref, inner_sem).wait()
        others.append(inner_stage_ref)
    rows, width = high_ref.shape
    extent = sum(ref.shape[0] for ref in others)
    triple = both_ref.shape[0] == 3 * extent

    def gather(at, cols, state):
        main, rest = state
        high, low = halves(jnp.concatenate([ref[:, cols] for ref in others], axis=0))
        both = jnp.concatenate([high, low], axis=0)
        both_ref[: 2 * extent, cols] = both
        if triple:
            both_ref[2 * extent :, cols] = high
        return main + mxu(high_ref[:, cols], both, NT), rest + mxu(low_ref[:, cols], high, NT)

    start = (jnp.zeros((rows, 2 * extent), jnp.float32), jnp.zeros((rows, extent), jnp.float32))
    main, rest = over_panels(width, gather, start, unroll)
    integral = main[:, :extent] + (main[:, extent:] + rest)
    gap_col = jnp.concatenate(
        [table_ref[row : row + 1, at : at + height] for row, at, height in gaps], axis=1
    )
    a_high, a_low = halves(integral / (gap_row_ref[...] + gap_col))
    a_twice = jnp.concatenate([a_high, a_high] + [a_low] * triple, axis=1)

    def spread(at, cols, state):
        both = both_ref[:, cols]
        gamma = mxu(a_twice, both)
        if not triple:
            gamma += mxu(a_low, both[:extent])
        gamma += start_ref[:, cols]
        if final:
            stage_ref, sem = refs
            stage_ref[:, cols] = gamma
            fetch(stage_ref.at[:, cols], gamma_ref.at[:, cols], sem.at[at])
        else:
            gamma_ref[:, cols] = gamma
        return state

    over_panels(width, spread, 0, unroll)
    if final:
        stage_ref, sem = refs
        for at, cols in enumerate(panels(width)):
            pltpu.make_async_copy(stage_ref.at[:, cols], gamma_ref.at[:, cols], sem.at[at]).wait()


VMEM = pl.BlockSpec(memory_space=pltpu.VMEM)
HBM = pl.BlockSpec(memory_space=pltpu.HBM)


def cost(rows, extent, width):
    return pl.CostEstimate(flops=12 * rows * extent * width, bytes_accessed=4 * extent * width, transcendentals=0)


def in_vmem(array):
    return pltpu.with_memory_space_constraint(array, pltpu.VMEM)


def in_hbm(array):
    return pltpu.with_memory_space_constraint(array, pltpu.HBM)


def params(mebibytes):
    return pltpu.CompilerParams(vmem_limit_bytes=mebibytes << 20)


def cut_call(mine, ranges):
    width = mine.shape[1]
    count = len(ranges)
    return pl.pallas_call(
        functools.partial(cut_kernel, [start for start, _ in ranges]),
        out_shape=tuple(pltpu.VMEM((height, width), jnp.float32) for _, height in ranges),
        in_specs=[HBM],
        out_specs=(VMEM,) * count,
        scratch_shapes=[pltpu.SemaphoreType.DMA((count,))],
        compiler_params=params(2),
        cost_estimate=pl.CostEstimate(flops=0, bytes_accessed=1 << 20, transcendentals=0),
        name="first_cuts",
    )(in_hbm(mine))


def split_call(mine, ranges):
    rows, width = mine.shape
    count = len(ranges)
    return pl.pallas_call(
        functools.partial(split_kernel, [start for start, _ in ranges]),
        out_shape=tuple(pltpu.HBM((height, width), jnp.float32) for _, height in ranges),
        in_specs=[HBM],
        out_specs=(HBM,) * count,
        scratch_shapes=[
            pltpu.VMEM((rows, width), jnp.float32),
            pltpu.SemaphoreType.DMA((count,)),
            pltpu.SemaphoreType.DMA((count,)),
        ],
        compiler_params=params(6),
        cost_estimate=cost(rows, rows, width),
        name="other_cuts",
    )(in_hbm(mine))


def own_call(mine, gap_row, gap_col):
    rows, width = mine.shape
    factor = pltpu.VMEM((rows, width), jnp.bfloat16)
    return pl.pallas_call(
        own_kernel,
        out_shape=(factor, factor, pltpu.VMEM((rows, width), jnp.float32)),
        in_specs=[HBM, VMEM, VMEM],
        out_specs=(VMEM,) * 3,
        scratch_shapes=[
            pltpu.VMEM((rows, width), jnp.float32),
            pltpu.SemaphoreType.DMA((width // PANEL,)),
        ],
        compiler_params=params(10),
        cost_estimate=pl.CostEstimate(flops=1 << 20, bytes_accessed=1 << 16, transcendentals=0),
        name="own_block",
    )(in_hbm(mine), gap_row, gap_col)


def step_call(others, high, low, gap_row, table, gaps, begin, inner, inner_rows, final, unroll, name):
    rows, width = high.shape
    extent = sum(other.shape[0] for other in others)
    scratch = []
    if inner_rows:
        extent += inner_rows[1]
        scratch += [pltpu.VMEM((inner_rows[1], width), jnp.float32), pltpu.SemaphoreType.DMA]
    if final:
        scratch += [pltpu.VMEM((rows, width), jnp.float32), pltpu.SemaphoreType.DMA((width // PANEL,))]
    pieces = 3 if 3 * extent <= rows else 2
    extra = [in_hbm(inner)] if inner_rows else []
    return pl.pallas_call(
        functools.partial(step_kernel, (len(others), inner_rows, gaps, final, unroll)),
        out_shape=(pltpu.HBM if final else pltpu.VMEM)((rows, width), jnp.float32),
        in_specs=[VMEM] * (len(others) + 5) + [HBM] * len(extra),
        out_specs=HBM if final else VMEM,
        scratch_shapes=[pltpu.VMEM((pieces * extent, width), jnp.bfloat16)] + scratch,
        input_output_aliases={} if final else {len(others) + 4: 0},
        compiler_params=params(10),
        cost_estimate=pl.CostEstimate(flops=1 << 20, bytes_accessed=1 << 16, transcendentals=0),
        name=name,
    )(*map(in_vmem, others), in_vmem(high), in_vmem(low), gap_row, table, in_vmem(begin), *extra)


def local(b_factors, occ_energy, vir_energy):
    occ_block, vir_block, width = b_factors.shape
    occ_count = lax.axis_size("occ")
    vir_count = lax.axis_size("vir")
    occ_here = lax.axis_index("occ")
    vir_here = lax.axis_index("vir")

    def moved(block, target):
        route = []
        for occ in range(occ_count):
            for vir in range(vir_count):
                occ_to, vir_to = target(occ, vir)
                route.append(
                    (occ * vir_count + vir, occ_to % occ_count * vir_count + vir_to % vir_count)
                )
        return lax.ppermute(block, AXES, route)

    def across(occ, vir):
        return occ ^ 1, vir

    def back(occ, vir):
        return (occ + 2 if occ % 2 else occ - 2), vir

    def along(occ, vir):
        return (occ - 2 if occ % 2 else occ + 2), vir

    def outward(occ, vir):
        return occ ^ 1, (vir + 1 if vir % 2 else vir - 1)

    def inward(occ, vir):
        return occ, vir ^ 1

    def gap_of(occ_place, vir_place):
        occ_part = lax.dynamic_slice_in_dim(
            occ_energy, occ_place % occ_count * occ_block, occ_block
        )
        vir_part = lax.dynamic_slice_in_dim(
            vir_energy, vir_place % vir_count * vir_block, vir_block
        )
        return occ_part[:, None] - vir_part[None, :]

    occ_side = 1 - 2 * (occ_here % 2)
    vir_side = 1 - 2 * (vir_here % 2)
    gap = gap_of(occ_here, vir_here)
    gap_inner = gap_of(occ_here, vir_here + vir_side)
    gap_near = gap_of(occ_here + occ_side, vir_here)
    gap_far = gap_of(occ_here + occ_count - occ_side, vir_here)
    gap_outer = gap_of(occ_here, vir_here + vir_count - vir_side)
    gap_row = gap.reshape(-1, 1)
    table = jnp.concatenate([gap_near, gap_far, gap_outer, gap_inner], axis=1)

    def held(value, *earlier):
        return lax.optimization_barrier((value, earlier))[0]

    mine = b_factors.reshape(occ_block * vir_block, width)
    size = mine.shape[0]
    early = vir_block // 2
    count = occ_block
    ranges = [(k * vir_block, vir_block) for k in range(count)]

    [first] = cut_call(mine, ranges[:1])
    parts = [first]
    near = [moved(first, across)]
    inner = moved(b_factors, inward).reshape(size, width)
    *rest, ahead = split_call(held(mine, first), ranges[1:] + [(size - early, early)])
    parts += rest
    near.append(moved(parts[1], across))
    ahead_back, ahead_out = moved(ahead, back), moved(ahead, outward)
    high, low, gamma = own_call(held(mine, near[0], inner), gap_row, gap.reshape(1, -1))

    done = [parts[1], gamma]
    far, outer = [], []
    begin = gamma
    inner_at = 0

    def step(k, *earlier):
        nonlocal begin, inner_at
        final = k == count - 1
        others = [near[k], far[k], outer[k]]
        rows = None
        if final:
            others = [far[k], outer[k], late]
            at = vir_block - early
            gaps = [(k, which * vir_block + shift, early) for shift in (0, at) for which in (1, 2)]
        else:
            others = [held(other, *earlier) for other in others]
            height = INNER_ROWS[k] * vir_block
            rows = (inner_at, height) if height else None
            gaps = [(k, 0, 3 * vir_block)]
            if k == count - 2:
                others.append(near[k + 1])
                gaps.append((k + 1, 0, vir_block))
            gaps += [(row, 3 * vir_block, vir_block) for row in range(inner_at // vir_block, (inner_at + height) // vir_block)]
            inner_at += height
        gamma = step_call(others, high, low, gap_row, table, gaps, begin, inner, rows, final, 4 if k > 3 else 2, "step_%d" % k)
        begin = gamma
        done.append(gamma)
        return gamma

    relayed = jnp.concatenate([ahead_back, ahead_out], axis=0)
    for k in range(count):
        part = held(near[k], done[k])
        if k == 0:
            part = held(part, ahead_back, ahead_out)
        if k == 1:
            part = held(part, relayed)
        if k == count - 1:
            part = part[: vir_block - early]
        far.append(moved(part, along))
        outer.append(moved(part, outward))
        if k + 2 < count:
            near.append(moved(held(parts[k + 2], part), across))
        elif k + 2 == count:
            late = moved(held(relayed, part, far[k - 1], outer[k - 1]), across)
        if k > 0:
            step(k - 1, part)
    gamma = step(count - 1)
    return gamma.reshape(occ_block, vir_block, width)


def solution(mesh):
    in_specs = (P("occ", "vir", None), P(), P())
    out_specs = P("occ", "vir", None)
    return jax.shard_map(local, mesh=mesh, in_specs=in_specs, out_specs=out_specs, check_vma=False)
```

```python
import functools
import jax
import jax.numpy as jnp
from jax import lax
from jax.experimental import pallas as pl
from jax.experimental.pallas import tpu as pltpu
from jax.sharding import PartitionSpec as P

AXES = ("occ", "vir")
PANEL = 1024
INNER_ROWS = (1, 1, 1, 1, 2, 2, 0)
NT = (((1,), (1,)), ((), ()))
NN = (((1,), (0,)), ((), ()))


def mxu(left, right, dims=NN):
    return lax.dot_general(left, right, dims, preferred_element_type=jnp.float32)


def halves(value):
    high = value.astype(jnp.bfloat16)
    low = (value - high.astype(jnp.float32)).astype(jnp.bfloat16)
    return high, low


def panels(width):
    return [slice(at, at + PANEL) for at in range(0, width, PANEL)]


def fetch(source_ref, target_ref, sem):
    copy = pltpu.make_async_copy(source_ref, target_ref, sem)
    copy.start()
    return copy


def row_cuts(mine_ref, targets, starts, sem):
    copies = []
    for at, (target, start) in enumerate(zip(targets, starts)):
        rows = pl.ds(start, target.shape[0])
        copies.append(fetch(mine_ref.at[rows], target, sem.at[at]))
    return copies


def cut_kernel(starts, mine_ref, *refs):
    for copy in row_cuts(mine_ref, refs[:-1], starts, refs[-1]):
        copy.wait()


def over_panels(width, body, start, unroll=2):
    def turn(at, state):
        return body(at, pl.ds(pl.multiple_of(at * PANEL, PANEL), PANEL), state)

    return lax.fori_loop(0, width // PANEL, turn, start, unroll=unroll)


def split_kernel(starts, mine_ref, *refs):
    *parts, stage_ref, in_sem, out_sem = refs
    arrivals, departures = [], []
    reached = starts[0]
    for at, (part, start) in enumerate(zip(parts, starts)):
        if start >= reached:
            reached = start + part.shape[0]
            rows = pl.ds(start, part.shape[0])
            arrivals.append(fetch(mine_ref.at[rows], stage_ref.at[rows], in_sem.at[at]))
    for at, (part, start) in enumerate(zip(parts, starts)):
        if at < len(arrivals):
            arrivals[at].wait()
        departures.append(fetch(stage_ref.at[pl.ds(start, part.shape[0])], part, out_sem.at[at]))
    for copy in departures:
        copy.wait()


def own_kernel(mine_ref, gap_row_ref, gap_col_ref, high_ref, low_ref, gamma_ref, stage_ref, sem):
    rows, width = mine_ref.shape
    for at, cols in enumerate(panels(width)):
        fetch(mine_ref.at[:, cols], stage_ref.at[:, cols], sem.at[at])

    def gather(at, cols, state):
        integral, cross = state
        pltpu.make_async_copy(mine_ref.at[:, cols], stage_ref.at[:, cols], sem.at[at]).wait()
        high, low = halves(stage_ref[:, cols])
        high_ref[:, cols] = high
        low_ref[:, cols] = low
        return integral + mxu(high, high, NT), cross + mxu(high, low, NT)

    zero = jnp.zeros((rows, rows), jnp.float32)
    integral, cross = over_panels(width, gather, (zero, zero))
    integral = integral + (cross + cross.T)
    a_high, a_low = halves(integral / (gap_row_ref[...] + gap_col_ref[...]))

    def spread(at, cols, state):
        high, low = high_ref[:, cols], low_ref[:, cols]
        gamma_ref[:, cols] = mxu(a_high, high) + (mxu(a_high, low) + mxu(a_low, high))
        return state

    over_panels(width, spread, 0)


def step_kernel(plan, *refs):
    count, inner_rows, gaps, final, unroll = plan
    refs = list(refs)
    take = lambda number: [refs.pop(0) for _ in range(number)]
    others = take(count)
    high_ref, low_ref, gap_row_ref, table_ref = take(4)
    start_ref = take(1)[0]
    inner_ref = take(1)[0] if inner_rows else None
    gamma_ref, both_ref = take(2)
    if inner_rows:
        inner_stage_ref, inner_sem = take(2)
        at, height = inner_rows
        fetch(inner_ref.at[pl.ds(at, height)], inner_stage_ref, inner_sem).wait()
        others.append(inner_stage_ref)
    rows, width = high_ref.shape
    extent = sum(ref.shape[0] for ref in others)
    triple = both_ref.shape[0] == 3 * extent
    row_halves = pl.ds(0, rows // 2), pl.ds(rows // 2, rows // 2)

    def gather(at, cols, state):
        main, rest = state
        high, low = halves(jnp.concatenate([ref[:, cols] for ref in others], axis=0))
        both = jnp.concatenate([high, low], axis=0)
        both_ref[: 2 * extent, cols] = both
        if triple:
            both_ref[2 * extent :, cols] = high
        return main + mxu(high_ref[:, cols], both, NT), rest + mxu(low_ref[:, cols], high, NT)

    start = (jnp.zeros((rows, 2 * extent), jnp.float32), jnp.zeros((rows, extent), jnp.float32))
    main, rest = over_panels(width, gather, start, unroll)
    integral = main[:, :extent] + (main[:, extent:] + rest)
    gap_col = jnp.concatenate(
        [table_ref[row : row + 1, at : at + height] for row, at, height in gaps], axis=1
    )
    a_high, a_low = halves(integral / (gap_row_ref[...] + gap_col))
    a_twice = jnp.concatenate([a_high, a_high] + [a_low] * triple, axis=1)

    def spread(at, cols, state):
        both = both_ref[:, cols]
        gamma = mxu(a_twice, both)
        if not triple:
            gamma += mxu(a_low, both[:extent])
        gamma += start_ref[:, cols]
        if final:
            stage_ref, sem = refs
            stage_ref[:, cols] = gamma
            for half, piece in enumerate(row_halves):
                fetch(stage_ref.at[piece, cols], gamma_ref.at[piece, cols], sem.at[2 * at + half])
        else:
            gamma_ref[:, cols] = gamma
        return state

    over_panels(width, spread, 0, unroll)
    if final:
        stage_ref, sem = refs
        for at, cols in enumerate(panels(width)):
            for half, piece in enumerate(row_halves):
                pltpu.make_async_copy(
                    stage_ref.at[piece, cols], gamma_ref.at[piece, cols], sem.at[2 * at + half]
                ).wait()


VMEM = pl.BlockSpec(memory_space=pltpu.VMEM)
HBM = pl.BlockSpec(memory_space=pltpu.HBM)


def cost(rows, extent, width):
    return pl.CostEstimate(flops=12 * rows * extent * width, bytes_accessed=4 * extent * width, transcendentals=0)


def in_vmem(array):
    return pltpu.with_memory_space_constraint(array, pltpu.VMEM)


def in_hbm(array):
    return pltpu.with_memory_space_constraint(array, pltpu.HBM)


def params(mebibytes):
    return pltpu.CompilerParams(vmem_limit_bytes=mebibytes << 20)


def cut_call(mine, ranges):
    width = mine.shape[1]
    count = len(ranges)
    return pl.pallas_call(
        functools.partial(cut_kernel, [start for start, _ in ranges]),
        out_shape=tuple(pltpu.VMEM((height, width), jnp.float32) for _, height in ranges),
        in_specs=[HBM],
        out_specs=(VMEM,) * count,
        scratch_shapes=[pltpu.SemaphoreType.DMA((count,))],
        compiler_params=params(2),
        cost_estimate=pl.CostEstimate(flops=0, bytes_accessed=1 << 20, transcendentals=0),
        name="first_cuts",
    )(in_hbm(mine))


def split_call(mine, ranges):
    rows, width = mine.shape
    count = len(ranges)
    return pl.pallas_call(
        functools.partial(split_kernel, [start for start, _ in ranges]),
        out_shape=tuple(pltpu.HBM((height, width), jnp.float32) for _, height in ranges),
        in_specs=[HBM],
        out_specs=(HBM,) * count,
        scratch_shapes=[
            pltpu.VMEM((rows, width), jnp.float32),
            pltpu.SemaphoreType.DMA((count,)),
            pltpu.SemaphoreType.DMA((count,)),
        ],
        compiler_params=params(6),
        cost_estimate=cost(rows, rows, width),
        name="other_cuts",
    )(in_hbm(mine))


def own_call(mine, gap_row, gap_col):
    rows, width = mine.shape
    factor = pltpu.VMEM((rows, width), jnp.bfloat16)
    return pl.pallas_call(
        own_kernel,
        out_shape=(factor, factor, pltpu.VMEM((rows, width), jnp.float32)),
        in_specs=[HBM, VMEM, VMEM],
        out_specs=(VMEM,) * 3,
        scratch_shapes=[
            pltpu.VMEM((rows, width), jnp.float32),
            pltpu.SemaphoreType.DMA((width // PANEL,)),
        ],
        compiler_params=params(10),
        cost_estimate=pl.CostEstimate(flops=1 << 20, bytes_accessed=1 << 16, transcendentals=0),
        name="own_block",
    )(in_hbm(mine), gap_row, gap_col)


def step_call(others, high, low, gap_row, table, gaps, begin, inner, inner_rows, final, unroll, name):
    rows, width = high.shape
    extent = sum(other.shape[0] for other in others)
    scratch = []
    if inner_rows:
        extent += inner_rows[1]
        scratch += [pltpu.VMEM((inner_rows[1], width), jnp.float32), pltpu.SemaphoreType.DMA]
    if final:
        scratch += [pltpu.VMEM((rows, width), jnp.float32), pltpu.SemaphoreType.DMA((2 * width // PANEL,))]
    pieces = 3 if 3 * extent <= rows else 2
    extra = [in_hbm(inner)] if inner_rows else []
    return pl.pallas_call(
        functools.partial(step_kernel, (len(others), inner_rows, gaps, final, unroll)),
        out_shape=(pltpu.HBM if final else pltpu.VMEM)((rows, width), jnp.float32),
        in_specs=[VMEM] * (len(others) + 5) + [HBM] * len(extra),
        out_specs=HBM if final else VMEM,
        scratch_shapes=[pltpu.VMEM((pieces * extent, width), jnp.bfloat16)] + scratch,
        input_output_aliases={} if final else {len(others) + 4: 0},
        compiler_params=params(10),
        cost_estimate=pl.CostEstimate(flops=1 << 20, bytes_accessed=1 << 16, transcendentals=0),
        name=name,
    )(*map(in_vmem, others), in_vmem(high), in_vmem(low), gap_row, table, in_vmem(begin), *extra)


def local(b_factors, occ_energy, vir_energy):
    occ_block, vir_block, width = b_factors.shape
    occ_count = lax.axis_size("occ")
    vir_count = lax.axis_size("vir")
    occ_here = lax.axis_index("occ")
    vir_here = lax.axis_index("vir")

    def moved(block, target):
        route = []
        for occ in range(occ_count):
            for vir in range(vir_count):
                occ_to, vir_to = target(occ, vir)
                route.append(
                    (occ * vir_count + vir, occ_to % occ_count * vir_count + vir_to % vir_count)
                )
        return lax.ppermute(block, AXES, route)

    def across(occ, vir):
        return occ ^ 1, vir

    def back(occ, vir):
        return (occ + 2 if occ % 2 else occ - 2), vir

    def along(occ, vir):
        return (occ - 2 if occ % 2 else occ + 2), vir

    def outward(occ, vir):
        return occ ^ 1, (vir + 1 if vir % 2 else vir - 1)

    def inward(occ, vir):
        return occ, vir ^ 1

    def gap_of(occ_place, vir_place):
        occ_part = lax.dynamic_slice_in_dim(
            occ_energy, occ_place % occ_count * occ_block, occ_block
        )
        vir_part = lax.dynamic_slice_in_dim(
            vir_energy, vir_place % vir_count * vir_block, vir_block
        )
        return occ_part[:, None] - vir_part[None, :]

    occ_side = 1 - 2 * (occ_here % 2)
    vir_side = 1 - 2 * (vir_here % 2)
    gap = gap_of(occ_here, vir_here)
    gap_inner = gap_of(occ_here, vir_here + vir_side)
    gap_near = gap_of(occ_here + occ_side, vir_here)
    gap_far = gap_of(occ_here + occ_count - occ_side, vir_here)
    gap_outer = gap_of(occ_here, vir_here + vir_count - vir_side)
    gap_row = gap.reshape(-1, 1)
    table = jnp.concatenate([gap_near, gap_far, gap_outer, gap_inner], axis=1)

    def held(value, *earlier):
        return lax.optimization_barrier((value, earlier))[0]

    mine = b_factors.reshape(occ_block * vir_block, width)
    size = mine.shape[0]
    early = vir_block // 2
    count = occ_block
    ranges = [(k * vir_block, vir_block) for k in range(count)]

    [first] = cut_call(mine, ranges[:1])
    parts = [first]
    near = [moved(first, across)]
    inner = moved(b_factors, inward).reshape(size, width)
    *rest, ahead = split_call(held(mine, first), ranges[1:] + [(size - early, early)])
    parts += rest
    near.append(moved(parts[1], across))
    ahead_back, ahead_out = moved(ahead, back), moved(ahead, outward)
    high, low, gamma = own_call(held(mine, near[0], inner), gap_row, gap.reshape(1, -1))

    done = [parts[1], gamma]
    far, outer = [], []
    begin = gamma
    inner_at = 0

    def step(k, *earlier):
        nonlocal begin, inner_at
        final = k == count - 1
        others = [near[k], far[k], outer[k]]
        rows = None
        if final:
            others = [far[k], outer[k], late]
            at = vir_block - early
            gaps = [(k, which * vir_block + shift, early) for shift in (0, at) for which in (1, 2)]
        else:
            others = [held(other, *earlier) for other in others]
            height = INNER_ROWS[k] * vir_block
            rows = (inner_at, height) if height else None
            gaps = [(k, 0, 3 * vir_block)]
            if k == count - 2:
                others.append(near[k + 1])
                gaps.append((k + 1, 0, vir_block))
            gaps += [(row, 3 * vir_block, vir_block) for row in range(inner_at // vir_block, (inner_at + height) // vir_block)]
            inner_at += height
        gamma = step_call(others, high, low, gap_row, table, gaps, begin, inner, rows, final, 4 if k > 3 else 2, "step_%d" % k)
        begin = gamma
        done.append(gamma)
        return gamma

    relayed = jnp.concatenate([ahead_back, ahead_out], axis=0)
    for k in range(count):
        part = held(near[k], done[k])
        if k == 0:
            part = held(part, ahead_back, ahead_out)
        if k == 1:
            part = held(part, relayed)
        if k == count - 1:
            part = part[: vir_block - early]
        far.append(moved(part, along))
        outer.append(moved(part, outward))
        if k + 2 < count:
            near.append(moved(held(parts[k + 2], part), across))
        elif k + 2 == count:
            late = moved(held(relayed, part, far[k - 1], outer[k - 1]), across)
        if k > 0:
            step(k - 1, part)
    gamma = step(count - 1)
    return gamma.reshape(occ_block, vir_block, width)


def solution(mesh):
    in_specs = (P("occ", "vir", None), P(), P())
    out_specs = P("occ", "vir", None)
    return jax.shard_map(local, mesh=mesh, in_specs=in_specs, out_specs=out_specs, check_vma=False)
```
